256 devices in a mesh: user: 32 (over z, x), item: 4 (over y), rep: 2 (over core).
Axes of the slice: x: 4, y: 4, z: 8, core: 2. Of those that a mesh axis runs over, the one named last changes fastest.
Arguments:
- item_factors: bfloat16 [131072, 256], P(('user', 'item'))
- user_factors: bfloat16 [4096, 256], P(('user', 'item', 'rep')), may hold values from -6 to 6
- strengths: bfloat16 [4096, 1024], P(('user', 'item', 'rep')), may hold values from 0.5 to 40
- requests: int32 [256, 128], P(('user', 'item', 'rep')), may hold values from -1 to 7, as said below
- user_slots: int32 [4096, 8], P(('user', 'item', 'rep')), may hold values from 0 to 127, as said below
Outputs:
- user_new: float32 [4096, 256], P(('user', 'item', 'rep'))
- item_partial: float32 [131072, 256], P(('user', 'item'))
The draws below stay inside these ranges and needn't reach their ends.
Inputs may be any that keep to these rules, and one draw needn't show every extreme that they name: `requests`: entry [d, o] names the one tile of owner o that device d reads, or is -1; every row has at least 8 entries that are not -1. `user_slots`: each row holds 8 different owners o, each with requests[u // 16, o] >= 0.
All inputs are finite; a program needn't handle non-finite values.
Results may differ from the reference program's by a relative error of at most 0.0051.
Values may be sent and summed in bfloat16 or wider, within the bound.
No kernel may reach another device: no remote copies, remote signals or barrier semaphores. Data moves between devices by JAX's collectives and lax.ppermute only.
A program may use at most 64 MiB of HBM per device.

```python
import math
import jax
import jax.numpy as jnp
from jax import lax

RANK = 256
TILE = 128
USERS_DEV = 16
TILES_OWN = 8
SLOTS_USER = 8
ITERS = 2
OWNERS = 128
ALL_DEVICES = 256
USERS = 4096
ITEMS = 131072
N_USER = 32
N_ITEM = 4
N_REP = 2


def asked_mask(key):
    key = jax.random.fold_in(key, 7)
    coin = jax.random.randint(key, (ALL_DEVICES, OWNERS), 0, 5) < 3
    rows = jnp.arange(ALL_DEVICES, dtype=jnp.int32)[:, None]
    cols = jnp.arange(OWNERS, dtype=jnp.int32)[None, :]
    forced = (cols - rows) % OWNERS < SLOTS_USER
    return coin | forced | (rows == 0)


def draw_item_factors(key, part):
    key = jax.random.fold_in(key, 3)
    first, second = jax.random.split(key, 2)
    column_scale = jnp.exp(jax.random.uniform(first, (RANK,), jnp.float32, math.log(0.1), 0.0))
    base = jax.random.normal(second, (ITEMS, RANK), jnp.float32)
    return (base * column_scale[None, :] * math.sqrt(RANK / ITEMS)).astype(jnp.bfloat16)


def draw_requests(key, part):
    asked = asked_mask(key)
    key = jax.random.fold_in(key, 11)
    chosen = jax.random.randint(key, (ALL_DEVICES, OWNERS), 0, TILES_OWN)
    return jnp.where(asked, chosen, -1).astype(jnp.int32)


def draw_user_slots(key, part):
    asked = asked_mask(key)
    key = jax.random.fold_in(key, 13)
    owner_of = jnp.arange(USERS, dtype=jnp.int32) // USERS_DEV
    usable = asked[owner_of].astype(jnp.int32)
    noise = jax.random.randint(key, (USERS, OWNERS), 0, 1024)
    scores = usable * 1048576 + noise * OWNERS + jnp.arange(OWNERS, dtype=jnp.int32)[None, :]
    picked = jax.lax.top_k(scores, SLOTS_USER)[1]
    return picked.astype(jnp.int32)


def steps_of(key, dims, pieces, low, top_value):
    factor_of, own = 1.0, jax.random.fold_in(key, 6)
    for dim, blocks in pieces:
        steps = jnp.exp(jax.random.uniform(jax.random.fold_in(own, dim), (blocks,), jnp.float32, low / len(pieces), top_value / len(pieces)))
        factor_of = factor_of * jnp.repeat(steps, dims[dim] // blocks).reshape([-1 if axis == dim else 1 for axis in range(len(dims))])
    return factor_of


def centred(own_key, shape, width, bound, cuts=(), kind=jnp.bfloat16):
    loudness = steps_of(own_key, shape, cuts, -0.22, 0.18) if cuts else 1.0
    entries = jax.random.normal(own_key, shape, jnp.float32) * width * loudness
    return jnp.minimum(jnp.maximum(entries, -bound), bound).astype(kind)


def setup_inputs(seed: int = 0) -> dict:
    streams_of = jax.random.split(jax.random.key(seed), 6)
    item_factors = draw_item_factors(jax.random.fold_in(streams_of[5], 71), 0)
    user_factors = centred(streams_of[1], (USERS, RANK), 1.0, 6.0, ((0, 256),))
    strengths = jnp.clip(jnp.exp(math.log(40.0) - 4.3820266 * jax.random.uniform(streams_of[2], (USERS, SLOTS_USER * TILE), jnp.float32) ** steps_of(streams_of[2], (USERS, SLOTS_USER * TILE), ((0, 256),), -0.2, 0.2)), 0.5, 40.0).astype(jnp.bfloat16)
    requests = draw_requests(jax.random.fold_in(streams_of[5], 71), 0)
    user_slots = draw_user_slots(jax.random.fold_in(streams_of[5], 71), 0)
    return {"item_factors": item_factors, "user_factors": user_factors, "strengths": strengths, "requests": requests, "user_slots": user_slots}


penalty = 1.0


def absorb(tiles, gram_matrix, start_rows, strengths, user_slots):
    users = start_rows.shape[0]
    owners = tiles.shape[0]
    factor_dim = tiles.shape[2]
    group = math.gcd(users, 16)
    count = users // group

    def one_group(inputs):
        begin_rows, weight_rows, slot_rows = inputs
        block = tiles[slot_rows].reshape(group, SLOTS_USER * TILE, factor_dim)
        weights = weight_rows.astype(jnp.float32)
        confidence = (1.0 + weights).astype(jnp.bfloat16)
        rhs = jnp.einsum("uj,ujr->ur", confidence, block, preferred_element_type=jnp.float32)

        def against(vectors):
            return jnp.einsum("ur,ujr->uj", vectors, block, preferred_element_type=jnp.float32)

        def operate(vectors):
            scaled = (weights * against(vectors.astype(jnp.bfloat16))).astype(jnp.bfloat16)
            gram_part = jnp.dot(vectors, gram_matrix, precision=lax.Precision.HIGHEST)
            back = jnp.einsum("uj,ujr->ur", scaled, block, preferred_element_type=jnp.float32)
            return gram_part + back + penalty * vectors

        solution = begin_rows.astype(jnp.float32)
        residual = rhs - operate(solution)
        direction = residual
        norm_now = jnp.sum(residual * residual, axis=1, keepdims=True)
        for sweep in range(ITERS):
            image = operate(direction)
            step_size = norm_now / jnp.sum(direction * image, axis=1, keepdims=True)
            solution = solution + step_size * direction
            residual = residual - step_size * image
            norm_next = jnp.sum(residual * residual, axis=1, keepdims=True)
            direction = residual + (norm_next / norm_now) * direction
            norm_now = norm_next
        solved_rounded = solution.astype(jnp.bfloat16)
        fitted = against(solved_rounded)
        coeffs = (confidence.astype(jnp.float32) - weights * fitted).astype(jnp.bfloat16)
        return solution, coeffs, solved_rounded

    solution, coeffs, solved_rounded = lax.map(one_group, (
        start_rows.reshape(count, group, factor_dim),
        strengths.reshape(count, group, SLOTS_USER * TILE),
        user_slots.reshape(count, group, SLOTS_USER)))
    solution = solution.reshape(users, factor_dim)
    solved_rounded = solved_rounded.reshape(users, factor_dim)
    coeffs = coeffs.reshape(users, SLOTS_USER, TILE)
    onehot = (user_slots[:, :, None] == jnp.arange(owners, dtype=jnp.int32)[None, None, :]).astype(jnp.bfloat16)
    spread_coeffs = jnp.einsum("uko,ukj->uoj", onehot, coeffs, preferred_element_type=jnp.float32)
    spread_coeffs = spread_coeffs.astype(jnp.bfloat16).reshape(users, owners * TILE)
    return solution, spread_coeffs, solved_rounded


def reference(item_factors, user_factors, strengths, requests, user_slots):
    table = item_factors.reshape(OWNERS, TILES_OWN, TILE, RANK)
    gram_matrix = jnp.dot(item_factors.T, item_factors, preferred_element_type=jnp.float32)
    devices = N_USER * N_ITEM * N_REP
    start_all = user_factors.reshape(devices, USERS_DEV, RANK)
    weight_all = strengths.reshape(devices, USERS_DEV, SLOTS_USER * TILE)
    slots_all = user_slots.reshape(devices, USERS_DEV, SLOTS_USER)
    tile_range = jnp.arange(TILES_OWN, dtype=jnp.int32)

    def one_device(totals, inputs):
        asked_tiles, start_rows, weight_rows, slot_rows = inputs
        chosen = jnp.clip(asked_tiles, 0, TILES_OWN - 1).astype(jnp.int32)
        present = (asked_tiles >= 0).astype(jnp.bfloat16)
        fetched = table[jnp.arange(OWNERS, dtype=jnp.int32), chosen] * present[:, None, None]
        solution, coeffs, solved_rounded = absorb(fetched, gram_matrix, start_rows, weight_rows, slot_rows)
        partial_value = lax.dot_general(coeffs, solved_rounded, (((0,), (0,)), ((), ())), preferred_element_type=jnp.float32)
        partial_value = partial_value.reshape(OWNERS, TILE, RANK)
        pick = (asked_tiles[:, None] == tile_range[None, :]).astype(jnp.float32)
        totals = totals + pick[:, :, None, None] * partial_value[:, None, :, :]
        return totals, solution

    start_totals = jnp.zeros((OWNERS, TILES_OWN, TILE, RANK), jnp.float32)
    totals, solved = lax.scan(one_device, start_totals, (requests, start_all, weight_all, slots_all))
    return solved.reshape(USERS, RANK), totals.reshape(ITEMS, RANK)
```

```python
import functools

import jax
import jax.numpy as jnp
from jax import lax
from jax.experimental import pallas as pl
from jax.experimental.pallas import tpu as pltpu
from jax.sharding import Mesh, PartitionSpec as P

TILE = 128
RANK = 256
USERS = 16
SLOTS = 8
NZ, NX, NY = 8, 4, 4
PLANE = NX * NY
LINE_USERS = NZ * USERS
PLANE_ITEMS = PLANE * TILE
PENALTY = 1.0
EVERY = ("z", "x", "y", "c")
BF, F32 = jnp.bfloat16, jnp.float32
HIGH = lax.Precision.HIGHEST
WIDE = SLOTS * TILE + RANK + 2 * TILE
EXTRA = 16
VMEM_LIMIT = 48 * 2**20


def ring_pairs(distance, phase):
    pairs = []
    for z in range(NZ):
        for x in range(NX):
            for y in range(NY):
                for c in range(2):
                    along_y = (c == 0) == (phase == 0)
                    x2 = x if along_y else (x + distance) % NX
                    y2 = (y + distance) % NY if along_y else y
                    pairs.append((((z * NX + x) * NY + y) * 2 + c, ((z * NX + x2) * NY + y2) * 2 + c))
    return pairs


def line_exchange(value):
    return [
        lax.ppermute(value, "z", [(s, (s + k) % NZ) for s in range(NZ)]) for k in range(1, NZ)
    ]


def swap_cores(value):
    return lax.ppermute(value, "c", [(0, 1), (1, 0)])


def against(vectors, block):
    return lax.dot_general(vectors, block, (((1,), (1,)), ((), ())), preferred_element_type=F32)


def load_tiles(tiles_hbm, tiles, sems):
    for s in range(NZ):
        rows = pl.ds(s * PLANE_ITEMS, PLANE_ITEMS)
        pltpu.make_async_copy(tiles_hbm.at[rows], tiles.at[rows], sems.at[s]).start()


def wait_tiles(tiles_hbm, tiles, sems, s):
    rows = pl.ds(s * PLANE_ITEMS, PLANE_ITEMS)
    pltpu.make_async_copy(tiles_hbm.at[rows], tiles.at[rows], sems.at[s]).wait()


def first_kernel(code_ref, row_ref, place_ref, pay_ref, gram_a, gram_b, *rest):
    sources = rest[:10]
    part_out, tiles_out, weights_out, start_out, tiles, sems, out_sems = rest[10:]
    z = place_ref[0]

    def visit(index, carry):
        s = lax.div(index, PLANE)
        code = code_ref[index]
        row = pl.multiple_of(row_ref[index] * TILE, TILE)
        target = tiles.at[pl.ds(pl.multiple_of(index * TILE, TILE), TILE)]
        for number in range(10):

            @pl.when(code == number)
            def _():
                pltpu.make_async_copy(
                    sources[number].at[pl.ds(row, TILE)], target, sems.at[s]
                ).start()

        return carry

    lax.fori_loop(0, NZ * PLANE, visit, 0)

    for s in range(NZ):
        place = lax.rem(s - z - 1 + 2 * NZ, NZ)
        rows = pl.ds(s * USERS, USERS)
        start_out[rows, :] = pay_ref[place, :, SLOTS * TILE : SLOTS * TILE + RANK].astype(F32)
        slots = pay_ref[place, :, SLOTS * TILE + RANK : SLOTS * TILE + RANK + TILE].astype(F32)
        owners = [jnp.broadcast_to(slots[:, k : k + 1], (USERS, TILE)) for k in range(SLOTS)]
        values = [pay_ref[place, :, k * TILE : (k + 1) * TILE].astype(F32) for k in range(SLOTS)]
        for j in range(PLANE):
            owner = (z * PLANE + j).astype(F32)
            total = jnp.zeros((USERS, TILE), F32)
            for k in range(SLOTS):
                total = jnp.where(owners[k] == owner, values[k], total)
            weights_out[rows, j * TILE : (j + 1) * TILE] = total.astype(BF)

    gram = gram_a[...] + gram_b[...]
    part_out[...] = -jnp.dot(start_out[...], gram, precision=HIGH, preferred_element_type=F32)
    for s in range(NZ):
        rows = pl.ds(s * USERS, USERS)
        here = pl.ds(s * PLANE_ITEMS, PLANE_ITEMS)
        pltpu.make_async_copy(tiles_out.at[here], tiles.at[here], sems.at[s]).wait()
        pltpu.make_async_copy(tiles.at[here], tiles_out.at[here], out_sems.at[s]).start()
        block = tiles[here, :]
        weights = weights_out[rows, :].astype(F32)
        confidence = jnp.where(weights > 0.0, 1.0 + weights, 0.0).astype(BF)
        scaled = (weights * against(start_out[rows, :].astype(BF), block)).astype(BF)
        both = jnp.dot(
            jnp.concatenate([confidence, scaled], axis=0), block, preferred_element_type=F32
        )
        part_out[rows, :] += both[:USERS] - both[USERS:]
    for s in range(NZ):
        here = pl.ds(s * PLANE_ITEMS, PLANE_ITEMS)
        pltpu.make_async_copy(tiles.at[here], tiles_out.at[here], out_sems.at[s]).wait()


def second_kernel(*refs):
    parts = refs[:NZ]
    start_ref, gram_a, gram_b, weights_ref, tiles_hbm, residual_out, part_out, tiles, sems = refs[NZ:]
    load_tiles(tiles_hbm, tiles, sems)
    residual = parts[0][...]
    for other in parts[1:]:
        residual = residual + other[...]
    residual = residual - PENALTY * start_ref[...]
    residual_out[...] = residual
    gram = gram_a[...] + gram_b[...]
    part_out[...] = jnp.dot(residual, gram, precision=HIGH, preferred_element_type=F32)
    for s in range(NZ):
        rows = pl.ds(s * USERS, USERS)
        wait_tiles(tiles_hbm, tiles, sems, s)
        block = tiles[pl.ds(s * PLANE_ITEMS, PLANE_ITEMS), :]
        weights = weights_ref[rows, :].astype(F32)
        scaled = (weights * against(residual_out[rows, :].astype(BF), block)).astype(BF)
        part_out[rows, :] += jnp.dot(scaled, block, preferred_element_type=F32)


def third_kernel(*refs):
    parts = refs[:NZ]
    (
        start_ref, residual_ref, gram_a, gram_b, weights_ref, tiles_hbm,
        value_out, direction_out, norm_out, curve_out, tiles, column, sems,
    ) = refs[NZ:]
    load_tiles(tiles_hbm, tiles, sems)
    direction = residual_ref[...]
    image = parts[0][...]
    for other in parts[1:]:
        image = image + other[...]
    image = image + PENALTY * direction
    norm_now = jnp.sum(direction * direction, axis=1, keepdims=True)
    step = norm_now / jnp.sum(direction * image, axis=1, keepdims=True)
    value_out[...] = start_ref[...] + step * direction
    residual = direction - step * image
    norm_next = jnp.sum(residual * residual, axis=1, keepdims=True)
    direction = residual + (norm_next / norm_now) * direction
    direction_out[...] = direction
    norm_out[...] = jnp.broadcast_to(norm_next, (LINE_USERS, TILE))
    gram = gram_a[...] + gram_b[...]
    image = jnp.dot(direction, gram, precision=HIGH, preferred_element_type=F32)
    column[...] = jnp.broadcast_to(
        jnp.sum(direction * image, axis=1, keepdims=True), (LINE_USERS, TILE)
    )
    for s in range(NZ):
        rows = pl.ds(s * USERS, USERS)
        wait_tiles(tiles_hbm, tiles, sems, s)
        block = tiles[pl.ds(s * PLANE_ITEMS, PLANE_ITEMS), :]
        weights = weights_ref[rows, :].astype(F32)
        fitted = against(direction_out[rows, :].astype(BF), block)
        scaled = (weights * fitted).astype(BF).astype(F32)
        column[rows, :] += jnp.broadcast_to(
            jnp.sum(scaled * fitted, axis=1, keepdims=True), (USERS, TILE)
        )
    curve_out[...] = column[...].T[:8, :]


def fourth_kernel(place_ref, *refs):
    parts = refs[:NZ]
    (
        value_ref, direction_ref, norm_ref, weights_ref, asked_ref, tiles_hbm,
        solved_out, send_out, tiles, solved, sems,
    ) = refs[NZ:]
    load_tiles(tiles_hbm, tiles, sems)
    z = place_ref[0]
    curve = parts[0][...]
    for other in parts[1:]:
        curve = curve + other[...]
    curve = jnp.broadcast_to(curve[:1, :], (TILE, LINE_USERS)).T[:, :1]
    direction = direction_ref[...]
    curve = curve + PENALTY * jnp.sum(direction * direction, axis=1, keepdims=True)
    step = norm_ref[:, :1] / curve
    solved[...] = value_ref[...] + step * direction
    solved_out[...] = solved[pl.ds(pl.multiple_of(z * USERS, USERS), USERS), :]
    for j in range(PLANE):
        send_out[j, LINE_USERS:, :] = jnp.zeros((EXTRA, TILE + RANK), BF)
        send_out[j, LINE_USERS:, :TILE] = jnp.broadcast_to(
            asked_ref[j : j + 1, :], (EXTRA, TILE)
        ).astype(BF)
    for s in range(NZ):
        rows = pl.ds(s * USERS, USERS)
        wait_tiles(tiles_hbm, tiles, sems, s)
        block = tiles[pl.ds(s * PLANE_ITEMS, PLANE_ITEMS), :]
        weights = weights_ref[rows, :].astype(F32)
        confidence = (1.0 + weights).astype(BF).astype(F32)
        rounded = solved[rows, :].astype(BF)
        coeffs = confidence - weights * against(rounded, block)
        coeffs = jnp.where(weights > 0.0, coeffs, 0.0).astype(BF)
        for j in range(PLANE):
            send_out[j, rows, :TILE] = coeffs[:, j * TILE : (j + 1) * TILE]
            send_out[j, rows, TILE:] = rounded


def owner_kernel(got_ref, out_ref, coeffs, rounded):
    for p in range(PLANE):
        coeffs[:, p * LINE_USERS : (p + 1) * LINE_USERS] = (
            got_ref[p, :LINE_USERS, :TILE].astype(F32).T
        )
        rounded[p * LINE_USERS : (p + 1) * LINE_USERS, :] = got_ref[p, :LINE_USERS, TILE:]
    asked = jnp.concatenate(
        [got_ref[p, LINE_USERS : LINE_USERS + 8, :TILE].astype(F32)[:1] for p in range(PLANE)], axis=1
    )
    for t in range(out_ref.shape[0] // TILE):
        picked = jnp.where(asked == float(t), coeffs[...], 0.0).astype(BF)
        out_ref[t * TILE : (t + 1) * TILE, :] = jnp.dot(
            picked, rounded[...], preferred_element_type=F32
        )


def call(kernel, outs, operands, spaces, out_spaces, scratch, prefetch=0):
    memory = {"v": pltpu.VMEM, "a": pl.ANY}
    return pl.pallas_call(
        kernel,
        out_shape=outs,
        grid_spec=pltpu.PrefetchScalarGridSpec(
            num_scalar_prefetch=prefetch,
            grid=(1,),
            in_specs=[spec(memory[m]) for m in spaces],
            out_specs=[spec(memory[m]) for m in out_spaces],
            scratch_shapes=scratch,
        ),
        compiler_params=pltpu.CompilerParams(vmem_limit_bytes=VMEM_LIMIT),
    )(*operands)


def spec(space):
    return pl.BlockSpec(memory_space=space)


def shards(item_factors, user_factors, strengths, requests, user_slots):
    z, x, y, c = (lax.axis_index(name) for name in EVERY)
    shape = jax.ShapeDtypeStruct
    pay = jnp.concatenate(
        [
            strengths,
            user_factors,
            jnp.pad(user_slots, ((0, 0), (0, TILE - SLOTS))).astype(BF),
            jnp.broadcast_to(requests, (USERS, TILE)).astype(BF),
        ],
        axis=1,
    )
    pays = jnp.stack(line_exchange(pay)[::-1] + [pay])

    half_rows = item_factors.shape[0] // 2
    half = lax.dynamic_slice_in_dim(item_factors, c * half_rows, half_rows, 0)
    near = jnp.concatenate(
        [half] + [lax.ppermute(half, EVERY, ring_pairs(d, 0)) for d in (1, -1, 2)], axis=0
    )
    up = lax.ppermute(near, EVERY, ring_pairs(1, 1))
    down = lax.ppermute(near, EVERY, ring_pairs(-1, 1))
    middle = near.shape[0] // 2
    far_a = lax.ppermute(up[:middle], EVERY, ring_pairs(1, 1))
    far_b = lax.ppermute(down[middle:], EVERY, ring_pairs(-1, 1))
    own = [near, up, down, far_a, far_b]
    other = [swap_cores(v) for v in own]
    gram_a = sum(
        lax.dot_general(v, v, (((0,), (0,)), ((), ())), preferred_element_type=F32) for v in own
    )
    gram_b = swap_cores(gram_a)

    asked = pays[:, 0, WIDE - TILE :].astype(F32)
    asked = lax.dynamic_slice(
        jnp.concatenate([asked, asked], axis=0), (NZ - 1 - z, z * PLANE), (NZ, PLANE)
    )
    asked_rows = jnp.repeat(asked.T, USERS, axis=1)
    tile = jnp.maximum(asked.astype(jnp.int32), 0)
    part_of = tile // 4
    j = jnp.arange(PLANE, dtype=jnp.int32)[None, :]
    along_x = (j // NY - x) % NX
    along_y = (j % NY - y) % NY
    first = jnp.where(part_of == 0, along_y, along_x)
    second = jnp.where(part_of == 0, along_x, along_y)

    def slot(delta):
        return jnp.where(delta == 3, 1, jnp.where(delta == 0, 0, delta + 1))

    first, second = slot(first), slot(second)
    code = jnp.where(second < 3, second, 3 + first // 2) + jnp.where(part_of == c, 0, 5)
    row = jnp.where(second < 3, first, first % 2) * 4 + tile % 4
    place = z[None].astype(jnp.int32)

    tiles_type = shape((NZ * PLANE_ITEMS, RANK), BF)
    tiles_scratch = pltpu.VMEM(tiles_type.shape, BF)
    sems = pltpu.SemaphoreType.DMA((NZ,))
    vectors = shape((LINE_USERS, RANK), F32)
    part, tiles, weights, start = call(
        first_kernel,
        [vectors, tiles_type, shape((LINE_USERS, PLANE_ITEMS), BF), vectors],
        [code.reshape(-1), row.reshape(-1), place, pays, gram_a, gram_b, *own, *other],
        "vvv" + "a" * 10,
        "vavv",
        [tiles_scratch, sems, sems],
        prefetch=3,
    )
    residual, part = call(
        second_kernel,
        [vectors, vectors],
        [part, *line_exchange(part), start, gram_a, gram_b, weights, tiles],
        "v" * 12 + "a",
        "vv",
        [tiles_scratch, sems],
    )
    value, direction, norm, curve = call(
        third_kernel,
        [vectors, vectors, shape((LINE_USERS, TILE), F32), shape((8, LINE_USERS), F32)],
        [part, *line_exchange(part), start, residual, gram_a, gram_b, weights, tiles],
        "v" * 13 + "a",
        "vvvv",
        [tiles_scratch, pltpu.VMEM((LINE_USERS, TILE), F32), sems],
    )
    solved, send = call(
        fourth_kernel,
        [shape((USERS, RANK), F32), shape((PLANE, LINE_USERS + EXTRA, TILE + RANK), BF)],
        [place, curve, *line_exchange(curve), value, direction, norm, weights, asked_rows, tiles],
        "v" * 13 + "a",
        "vv",
        [tiles_scratch, pltpu.VMEM((LINE_USERS, RANK), F32), sems],
        prefetch=1,
    )
    got = lax.all_to_all(send, ("x", "y"), split_axis=0, concat_axis=0, tiled=True)
    [sums] = call(
        owner_kernel,
        [shape(item_factors.shape, F32)],
        [got],
        "v",
        "v",
        [
            pltpu.VMEM((TILE, PLANE * LINE_USERS), F32),
            pltpu.VMEM((PLANE * LINE_USERS, RANK), BF),
        ],
    )
    return solved, sums + swap_cores(sums)


def solution(mesh):
    cut = Mesh(mesh.devices.reshape(NZ, NX, NY, 2), EVERY)
    every, owner = P(EVERY, None), P(("z", "x", "y"), None)
    return jax.shard_map(
        shards,
        mesh=cut,
        in_specs=(owner, every, every, every, every),
        out_specs=(every, owner),
        check_vma=False,
    )
```

```python
import functools

import jax
import jax.numpy as jnp
from jax import lax
from jax.experimental import pallas as pl
from jax.experimental.pallas import tpu as pltpu
from jax.sharding import Mesh, PartitionSpec as P

TILE = 128
RANK = 256
USERS = 16
SLOTS = 8
NZ, NX, NY = 8, 4, 4
PLANE = NX * NY
LINE_USERS = NZ * USERS
PLANE_ITEMS = PLANE * TILE
PENALTY = 1.0
EVERY = ("z", "x", "y", "c")
BF, F32 = jnp.bfloat16, jnp.float32
HIGH = lax.Precision.HIGHEST
WIDE = SLOTS * TILE + RANK + 2 * TILE
EXTRA = 16
VMEM_LIMIT = 16 * 2**20
HALF = LINE_USERS // 2


def ring_pairs(distance, phase):
    pairs = []
    for z in range(NZ):
        for x in range(NX):
            for y in range(NY):
                for c in range(2):
                    along_y = (c == 0) == (phase == 0)
                    x2 = x if along_y else (x + distance) % NX
                    y2 = (y + distance) % NY if along_y else y
                    pairs.append((((z * NX + x) * NY + y) * 2 + c, ((z * NX + x2) * NY + y2) * 2 + c))
    return pairs


def line_permute(value, partner):
    return lax.ppermute(value, "z", [(s, partner(s)) for s in range(NZ)])


def line_gather(value):
    for k in (1, 2, 4):
        value = jnp.concatenate([value, line_permute(value, lambda s: s ^ k)], axis=0)
    return value


def line_sum(keep, give):
    mine = keep + line_permute(give, lambda s: s ^ 1)
    others = [line_permute(mine, lambda s: (s + k) % NZ) for k in (2, 4, 6)]
    total = mine + others[0] + others[1] + others[2]
    return total, line_permute(total, lambda s: s ^ 1)


def split_halves(place_ref, part, keep_out, give_out):
    side = lax.rem(place_ref[0], 2)
    keep_out[...] = part[pl.ds(pl.multiple_of(side * HALF, HALF), HALF), :]
    give_out[...] = part[pl.ds(pl.multiple_of((1 - side) * HALF, HALF), HALF), :]


def join_halves(place_ref, mine_ref, other_ref, part):
    side = lax.rem(place_ref[0], 2)
    part[pl.ds(pl.multiple_of(side * HALF, HALF), HALF), :] = mine_ref[...]
    part[pl.ds(pl.multiple_of((1 - side) * HALF, HALF), HALF), :] = other_ref[...]


def swap_cores(value):
    return lax.ppermute(value, "c", [(0, 1), (1, 0)])


def against(vectors, block):
    return lax.dot_general(vectors, block, (((1,), (1,)), ((), ())), preferred_element_type=F32)


def weights_kernel(place_ref, pay_ref, weights_out, start_out, asked_out):
    z = place_ref[0]
    for s in range(NZ):
        place = lax.bitwise_xor(z, s)
        rows = pl.ds(s * USERS, USERS)
        start_out[rows, :] = pay_ref[place, :, SLOTS * TILE : SLOTS * TILE + RANK].astype(F32)
        slots = pay_ref[place, :, SLOTS * TILE + RANK : SLOTS * TILE + RANK + TILE].astype(F32)
        asked_out[s : s + 1, :] = pay_ref[place, :, WIDE - TILE :].astype(F32)[:1]
        owners = [jnp.broadcast_to(slots[:, k : k + 1], (USERS, TILE)) for k in range(SLOTS)]
        values = [pay_ref[place, :, k * TILE : (k + 1) * TILE].astype(F32) for k in range(SLOTS)]
        for j in range(PLANE):
            owner = (z * PLANE + j).astype(F32)
            total = jnp.zeros((USERS, TILE), F32)
            for k in range(SLOTS):
                total = jnp.where(owners[k] == owner, values[k], total)
            weights_out[rows, j * TILE : (j + 1) * TILE] = total.astype(BF)


def first_kernel(code_ref, row_ref, place_ref, start_ref, weights_ref, gram_a, gram_b, *rest):
    sources = rest[:10]
    keep_out, give_out, tiles, part, sems = rest[10:]

    def visit(index, carry):
        s = lax.div(index, PLANE)
        code = code_ref[index]
        row = pl.multiple_of(row_ref[index] * TILE, TILE)
        target = tiles.at[pl.ds(pl.multiple_of(index * TILE, TILE), TILE)]

        def choose(low, high):
            if high - low == 1:
                pltpu.make_async_copy(sources[low].at[pl.ds(row, TILE)], target, sems.at[s]).start()
                return
            middle = (low + high) // 2
            lax.cond(code < middle, lambda: choose(low, middle), lambda: choose(middle, high))

        choose(0, 10)
        return carry

    lax.fori_loop(0, NZ * PLANE, visit, 0)
    gram = gram_a[...] + gram_b[...]
    part[...] = -jnp.dot(start_ref[...], gram, precision=HIGH, preferred_element_type=F32)
    for s in range(NZ):
        rows = pl.ds(s * USERS, USERS)
        here = pl.ds(s * PLANE_ITEMS, PLANE_ITEMS)
        pltpu.make_async_copy(sources[0], tiles.at[here], sems.at[s]).wait()
        block = tiles[here, :]
        weights = weights_ref[rows, :].astype(F32)
        confidence = jnp.where(weights > 0.0, 1.0 + weights, 0.0).astype(BF)
        scaled = (weights * against(start_ref[rows, :].astype(BF), block)).astype(BF)
        both = jnp.dot(
            jnp.concatenate([confidence, scaled], axis=0), block, preferred_element_type=F32
        )
        part[rows, :] += both[:USERS] - both[USERS:]
    split_halves(place_ref, part, keep_out, give_out)


def second_kernel(
    place_ref, mine_ref, other_ref, start_ref, gram_a, gram_b, weights_ref, tiles,
    residual_out, keep_out, give_out, part,
):
    join_halves(place_ref, mine_ref, other_ref, residual_out)
    residual = residual_out[...] - PENALTY * start_ref[...]
    residual_out[...] = residual
    gram = gram_a[...] + gram_b[...]
    part[...] = jnp.dot(residual, gram, precision=HIGH, preferred_element_type=F32)
    for s in range(NZ):
        rows = pl.ds(s * USERS, USERS)
        block = tiles[pl.ds(s * PLANE_ITEMS, PLANE_ITEMS), :]
        weights = weights_ref[rows, :].astype(F32)
        scaled = (weights * against(residual_out[rows, :].astype(BF), block)).astype(BF)
        part[rows, :] += jnp.dot(scaled, block, preferred_element_type=F32)
    split_halves(place_ref, part, keep_out, give_out)


def third_kernel(
    place_ref, mine_ref, other_ref, start_ref, residual_ref, gram_a, gram_b, weights_ref, tiles,
    value_out, direction_out, norm_out, curve_out, part, column,
):
    join_halves(place_ref, mine_ref, other_ref, part)
    direction = residual_ref[...]
    image = part[...] + PENALTY * direction
    norm_now = jnp.sum(direction * direction, axis=1, keepdims=True)
    step = norm_now / jnp.sum(direction * image, axis=1, keepdims=True)
    value_out[...] = start_ref[...] + step * direction
    residual = direction - step * image
    norm_next = jnp.sum(residual * residual, axis=1, keepdims=True)
    direction = residual + (norm_next / norm_now) * direction
    direction_out[...] = direction
    norm_out[...] = jnp.broadcast_to(norm_next, (LINE_USERS, TILE))
    gram = gram_a[...] + gram_b[...]
    image = jnp.dot(direction, gram, precision=HIGH, preferred_element_type=F32)
    column[...] = jnp.broadcast_to(
        jnp.sum(direction * image, axis=1, keepdims=True), (LINE_USERS, TILE)
    )
    for s in range(NZ):
        rows = pl.ds(s * USERS, USERS)
        block = tiles[pl.ds(s * PLANE_ITEMS, PLANE_ITEMS), :]
        weights = weights_ref[rows, :].astype(F32)
        fitted = against(direction_out[rows, :].astype(BF), block)
        scaled = (weights * fitted).astype(BF).astype(F32)
        column[rows, :] += jnp.broadcast_to(
            jnp.sum(scaled * fitted, axis=1, keepdims=True), (USERS, TILE)
        )
    curve_out[...] = column[...].T[:8, :]


def fourth_kernel(
    place_ref, curve_ref, value_ref, direction_ref, norm_ref, weights_ref, asked_ref, tiles,
    solved_out, send_out, solved,
):
    z = place_ref[0]
    curve = jnp.broadcast_to(curve_ref[:1, :], (TILE, LINE_USERS)).T[:, :1]
    direction = direction_ref[...]
    curve = curve + PENALTY * jnp.sum(direction * direction, axis=1, keepdims=True)
    step = norm_ref[:, :1] / curve
    solved[...] = value_ref[...] + step * direction
    solved_out[...] = solved[pl.ds(pl.multiple_of(z * USERS, USERS), USERS), :]
    for j in range(PLANE):
        send_out[j, LINE_USERS:, :] = jnp.zeros((EXTRA, TILE + RANK), BF)
        send_out[j, LINE_USERS:, :TILE] = jnp.broadcast_to(
            asked_ref[j : j + 1, :], (EXTRA, TILE)
        ).astype(BF)
    for s in range(NZ):
        rows = pl.ds(s * USERS, USERS)
        block = tiles[pl.ds(s * PLANE_ITEMS, PLANE_ITEMS), :]
        weights = weights_ref[rows, :].astype(F32)
        confidence = (1.0 + weights).astype(BF).astype(F32)
        rounded = solved[rows, :].astype(BF)
        coeffs = confidence - weights * against(rounded, block)
        coeffs = jnp.where(weights > 0.0, coeffs, 0.0).astype(BF)
        for j in range(PLANE):
            send_out[j, rows, :TILE] = coeffs[:, j * TILE : (j + 1) * TILE]
            send_out[j, rows, TILE:] = rounded


def owner_kernel(got_ref, out_ref, coeffs, rounded):
    for p in range(PLANE):
        coeffs[:, p * LINE_USERS : (p + 1) * LINE_USERS] = (
            got_ref[p, :LINE_USERS, :TILE].astype(F32).T
        )
        rounded[p * LINE_USERS : (p + 1) * LINE_USERS, :] = got_ref[p, :LINE_USERS, TILE:]
    asked = jnp.concatenate(
        [got_ref[p, LINE_USERS : LINE_USERS + 8, :TILE].astype(F32)[:1] for p in range(PLANE)], axis=1
    )
    for t in range(out_ref.shape[0] // TILE):
        picked = jnp.where(asked == float(t), coeffs[...], 0.0).astype(BF)
        out_ref[t * TILE : (t + 1) * TILE, :] = jnp.dot(
            picked, rounded[...], preferred_element_type=F32
        )


def call(kernel, outs, operands, spaces, out_spaces, scratch, prefetch=0):
    memory = {"v": pltpu.VMEM, "a": pl.ANY}
    return pl.pallas_call(
        kernel,
        out_shape=outs,
        grid_spec=pltpu.PrefetchScalarGridSpec(
            num_scalar_prefetch=prefetch,
            grid=(1,),
            in_specs=[spec(memory[m]) for m in spaces],
            out_specs=[spec(memory[m]) for m in out_spaces],
            scratch_shapes=scratch,
        ),
        compiler_params=pltpu.CompilerParams(vmem_limit_bytes=VMEM_LIMIT),
    )(*operands)


def spec(space):
    return pl.BlockSpec(memory_space=space)


def shards(item_factors, user_factors, strengths, requests, user_slots):
    z, x, y, c = (lax.axis_index(name) for name in EVERY)
    shape = jax.ShapeDtypeStruct
    pay = jnp.concatenate(
        [
            strengths,
            user_factors,
            jnp.pad(user_slots, ((0, 0), (0, TILE - SLOTS))).astype(BF),
            jnp.broadcast_to(requests, (USERS, TILE)).astype(BF),
        ],
        axis=1,
    )
    half_rows = item_factors.shape[0] // 2
    half = lax.dynamic_slice_in_dim(item_factors, c * half_rows, half_rows, 0)
    near = jnp.concatenate(
        [half] + [lax.ppermute(half, EVERY, ring_pairs(d, 0)) for d in (1, -1, 2)], axis=0
    )
    near, pay = lax.optimization_barrier((near, pay))
    pays = line_gather(pay[None])
    up = lax.ppermute(near, EVERY, ring_pairs(1, 1))
    down = lax.ppermute(near, EVERY, ring_pairs(-1, 1))
    middle = near.shape[0] // 2
    far_a = lax.ppermute(up[:middle], EVERY, ring_pairs(1, 1))
    far_b = lax.ppermute(down[middle:], EVERY, ring_pairs(-1, 1))
    own = [near, up, down, far_a, far_b]
    other = [swap_cores(v) for v in own]
    gram_a = sum(
        lax.dot_general(v, v, (((0,), (0,)), ((), ())), preferred_element_type=F32) for v in own
    )
    gram_b = swap_cores(gram_a)

    place = z[None].astype(jnp.int32)
    vectors = shape((LINE_USERS, RANK), F32)
    halves = shape((HALF, RANK), F32)
    weights, start, asked = call(
        weights_kernel,
        [shape((LINE_USERS, PLANE_ITEMS), BF), vectors, shape((NZ, TILE), F32)],
        [place, pays],
        "v",
        "vvv",
        [],
        prefetch=1,
    )
    asked = lax.dynamic_slice(asked, (0, z * PLANE), (NZ, PLANE))
    asked_rows = jnp.repeat(asked.T, USERS, axis=1)
    tile = jnp.maximum(asked.astype(jnp.int32), 0)
    part_of = tile // 4
    j = jnp.arange(PLANE, dtype=jnp.int32)[None, :]
    along_x = (j // NY - x) % NX
    along_y = (j % NY - y) % NY
    first = jnp.where(part_of == 0, along_y, along_x)
    second = jnp.where(part_of == 0, along_x, along_y)

    def slot(delta):
        return jnp.where(delta == 3, 1, jnp.where(delta == 0, 0, delta + 1))

    first, second = slot(first), slot(second)
    code = jnp.where(second < 3, second, 3 + first // 2) + jnp.where(part_of == c, 0, 5)
    row = jnp.where(second < 3, first, first % 2) * 4 + tile % 4
    part = pltpu.VMEM(vectors.shape, F32)
    keep, give, tiles = call(
        first_kernel,
        [halves, halves, shape((NZ * PLANE_ITEMS, RANK), BF)],
        [code.reshape(-1), row.reshape(-1), place, start, weights, gram_a, gram_b, *own, *other],
        "vvvv" + "a" * 10,
        "vvv",
        [part, pltpu.SemaphoreType.DMA((NZ,))],
        prefetch=3,
    )
    residual, keep, give = call(
        second_kernel,
        [vectors, halves, halves],
        [place, *line_sum(keep, give), start, gram_a, gram_b, weights, tiles],
        "v" * 7,
        "vvv",
        [part],
        prefetch=1,
    )
    value, direction, norm, curve = call(
        third_kernel,
        [vectors, vectors, shape((LINE_USERS, TILE), F32), shape((8, LINE_USERS), F32)],
        [place, *line_sum(keep, give), start, residual, gram_a, gram_b, weights, tiles],
        "v" * 8,
        "vvvv",
        [part, pltpu.VMEM((LINE_USERS, TILE), F32)],
        prefetch=1,
    )
    for k in (1, 2, 4):
        curve = curve + line_permute(curve, lambda s: s ^ k)
    solved, send = call(
        fourth_kernel,
        [shape((USERS, RANK), F32), shape((PLANE, LINE_USERS + EXTRA, TILE + RANK), BF)],
        [place, curve, value, direction, norm, weights, asked_rows, tiles],
        "v" * 7,
        "vv",
        [part],
        prefetch=1,
    )
    got = lax.all_to_all(send, ("x", "y"), split_axis=0, concat_axis=0, tiled=True)
    [sums] = call(
        owner_kernel,
        [shape(item_factors.shape, F32)],
        [got],
        "v",
        "v",
        [
            pltpu.VMEM((TILE, PLANE * LINE_USERS), F32),
            pltpu.VMEM((PLANE * LINE_USERS, RANK), BF),
        ],
    )
    return solved, sums + swap_cores(sums)


def solution(mesh):
    cut = Mesh(mesh.devices.reshape(NZ, NX, NY, 2), EVERY)
    every, owner = P(EVERY, None), P(("z", "x", "y"), None)
    return jax.shard_map(
        shards,
        mesh=cut,
        in_specs=(owner, every, every, every, every),
        out_specs=(every, owner),
        check_vma=False,
    )
```

```python
import functools

import jax
import jax.numpy as jnp
from jax import lax
from jax.experimental import pallas as pl
from jax.experimental.pallas import tpu as pltpu
from jax.sharding import Mesh, PartitionSpec as P

TILE = 128
RANK = 256
USERS = 16
SLOTS = 8
NZ, NX, NY = 8, 4, 4
PLANE = NX * NY
LINE_USERS = NZ * USERS
PLANE_ITEMS = PLANE * TILE
PENALTY = 1.0
EVERY = ("z", "x", "y", "c")
BF, F32 = jnp.bfloat16, jnp.float32
HIGH = lax.Precision.HIGHEST
WIDE = SLOTS * TILE + RANK + 2 * TILE
EXTRA = 16
VMEM_LIMIT = 16 * 2**20
HALF = LINE_USERS // 2
BLOCKS, BLOCK_ROWS = 6, 1024
SEND_ROWS = 3 * LINE_USERS + EXTRA


def ring_pairs(distance, phase):
    pairs = []
    for z in range(NZ):
        for x in range(NX):
            for y in range(NY):
                for c in range(2):
                    along_y = (c == 0) == (phase == 0)
                    x2 = x if along_y else (x + distance) % NX
                    y2 = (y + distance) % NY if along_y else y
                    pairs.append((((z * NX + x) * NY + y) * 2 + c, ((z * NX + x2) * NY + y2) * 2 + c))
    return pairs


def line_permute(value, partner):
    return lax.ppermute(value, "z", [(s, partner(s)) for s in range(NZ)])


def line_sum(keep, give):
    mine = keep + line_permute(give, lambda s: s ^ 1)
    others = [line_permute(mine, lambda s: (s + k) % NZ) for k in (2, 4, 6)]
    total = mine + others[0] + others[1] + others[2]
    return total, line_permute(total, lambda s: s ^ 1)


def split_halves(place_ref, part, keep_out, give_out):
    side = lax.rem(place_ref[0], 2)
    keep_out[...] = part[pl.ds(pl.multiple_of(side * HALF, HALF), HALF), :]
    give_out[...] = part[pl.ds(pl.multiple_of((1 - side) * HALF, HALF), HALF), :]


def join_halves(place_ref, mine_ref, other_ref, part):
    side = lax.rem(place_ref[0], 2)
    part[pl.ds(pl.multiple_of(side * HALF, HALF), HALF), :] = mine_ref[...]
    part[pl.ds(pl.multiple_of((1 - side) * HALF, HALF), HALF), :] = other_ref[...]


def swap_cores(value):
    return lax.ppermute(value, "c", [(0, 1), (1, 0)])


def against(vectors, block):
    return lax.dot_general(vectors, block, (((1,), (1,)), ((), ())), preferred_element_type=F32)


def tiles_of(row_ref, table, s):
    return jnp.concatenate(
        [
            table[pl.ds(pl.multiple_of(row_ref[s * PLANE + j] * TILE, TILE), TILE), :]
            for j in range(PLANE)
        ],
        axis=0,
    )


def weights_kernel(place_ref, held_ref, got_ref, weights_out, start_out, asked_out, lanes_out, wide):
    z = place_ref[0]
    for s in range(NZ):
        gap = lax.bitwise_xor(z, s)
        pair = lax.div(gap, 2)
        place = jnp.where(pair == 3, 1, jnp.where(pair == 0, 0, pair + 1))
        near = lax.bitwise_and(gap, 1) == 0

        def pay(start, stop):
            held = held_ref[place, :, start:stop].astype(F32)
            return jnp.where(near, held, got_ref[place, :, start:stop].astype(F32))

        rows = pl.ds(s * USERS, USERS)
        start_out[rows, :] = pay(SLOTS * TILE, SLOTS * TILE + RANK)
        slots = pay(SLOTS * TILE + RANK, SLOTS * TILE + RANK + TILE)
        asked = pay(WIDE - TILE, WIDE)
        asked_out[s : s + 1, :] = asked[:1]
        wide[rows, :] = asked
        owners = [jnp.broadcast_to(slots[:, k : k + 1], (USERS, TILE)) for k in range(SLOTS)]
        values = [pay(k * TILE, (k + 1) * TILE) for k in range(SLOTS)]
        for j in range(PLANE):
            owner = (z * PLANE + j).astype(F32)
            total = jnp.zeros((USERS, TILE), F32)
            for k in range(SLOTS):
                total = jnp.where(owners[k] == owner, values[k], total)
            weights_out[rows, j * TILE : (j + 1) * TILE] = total.astype(BF)
    wide[...] = wide[...].T
    lanes_out[...] = wide[pl.ds(pl.multiple_of(z * PLANE, PLANE), PLANE), :]


def gram_of(block):
    return lax.dot_general(block, block, (((0,), (0,)), ((), ())), preferred_element_type=F32)


def near_kernel(near_a, near_b, after_ref, later_a, later_b, gram_out):
    later_a[...] = near_a[...]
    later_b[...] = near_b[...]
    gram_out[...] = gram_of(near_a[...]) + gram_of(near_b[...])


def rest_kernel(*refs):
    sources, (after_ref, table, sems) = refs[:6], refs[6:]
    copies = [
        pltpu.make_async_copy(
            sources[i], table.at[pl.ds(i * BLOCK_ROWS, BLOCK_ROWS)], sems.at[i]
        )
        for i in range(6)
    ]
    for copy in copies:
        copy.start()
    for copy in copies:
        copy.wait()


def gram_kernel(gram_ref, table, gram_out):
    gram = gram_ref[...]
    for i in range(table.shape[0] // BLOCK_ROWS):
        gram = gram + gram_of(table[i * BLOCK_ROWS : (i + 1) * BLOCK_ROWS, :])
    gram_out[...] = gram


def first_kernel(row_ref, place_ref, start_ref, weights_ref, gram_a, gram_b, *rest):
    sources = rest[:BLOCKS]
    keep_out, give_out, gram_out, table, part, sems = rest[BLOCKS:]
    copies, row = [], 0
    for i, source in enumerate(sources):
        to = table.at[pl.ds(row, source.shape[0])]
        copies.append(pltpu.make_async_copy(source, to, sems.at[i]))
        row += source.shape[0]
    for copy in copies:
        copy.start()
    for copy in copies:
        copy.wait()
    gram = gram_a[...] + gram_b[...]
    gram_out[...] = gram
    part[...] = -jnp.dot(start_ref[...], gram, precision=HIGH, preferred_element_type=F32)
    for s in range(NZ):
        rows = pl.ds(s * USERS, USERS)
        block = tiles_of(row_ref, table, s)
        weights = weights_ref[rows, :].astype(F32)
        confidence = jnp.where(weights > 0.0, 1.0 + weights, 0.0).astype(BF)
        scaled = (weights * against(start_ref[rows, :].astype(BF), block)).astype(BF)
        both = jnp.dot(
            jnp.concatenate([confidence, scaled], axis=0), block, preferred_element_type=F32
        )
        part[rows, :] += both[:USERS] - both[USERS:]
    split_halves(place_ref, part, keep_out, give_out)


def second_kernel(
    row_ref, place_ref, mine_ref, other_ref, start_ref, gram_ref, weights_ref, table,
    residual_out, keep_out, give_out, part,
):
    join_halves(place_ref, mine_ref, other_ref, residual_out)
    residual = residual_out[...] - PENALTY * start_ref[...]
    residual_out[...] = residual
    part[...] = jnp.dot(residual, gram_ref[...], precision=HIGH, preferred_element_type=F32)
    for s in range(NZ):
        rows = pl.ds(s * USERS, USERS)
        block = tiles_of(row_ref, table, s)
        weights = weights_ref[rows, :].astype(F32)
        scaled = (weights * against(residual_out[rows, :].astype(BF), block)).astype(BF)
        part[rows, :] += jnp.dot(scaled, block, preferred_element_type=F32)
    split_halves(place_ref, part, keep_out, give_out)


def third_kernel(
    row_ref, place_ref, mine_ref, other_ref, start_ref, residual_ref, gram_ref, weights_ref, table,
    value_out, direction_out, norm_out, curve_out, part, column,
):
    join_halves(place_ref, mine_ref, other_ref, part)
    direction = residual_ref[...]
    image = part[...] + PENALTY * direction
    norm_now = jnp.sum(direction * direction, axis=1, keepdims=True)
    step = norm_now / jnp.sum(direction * image, axis=1, keepdims=True)
    value_out[...] = start_ref[...] + step * direction
    residual = direction - step * image
    norm_next = jnp.sum(residual * residual, axis=1, keepdims=True)
    direction = residual + (norm_next / norm_now) * direction
    direction_out[...] = direction
    norm_out[...] = jnp.broadcast_to(norm_next, (LINE_USERS, TILE))
    image = jnp.dot(direction, gram_ref[...], precision=HIGH, preferred_element_type=F32)
    column[...] = jnp.broadcast_to(
        jnp.sum(direction * image, axis=1, keepdims=True), (LINE_USERS, TILE)
    )
    for s in range(NZ):
        rows = pl.ds(s * USERS, USERS)
        block = tiles_of(row_ref, table, s)
        weights = weights_ref[rows, :].astype(F32)
        fitted = against(direction_out[rows, :].astype(BF), block)
        scaled = (weights * fitted).astype(BF).astype(F32)
        column[rows, :] += jnp.broadcast_to(
            jnp.sum(scaled * fitted, axis=1, keepdims=True), (USERS, TILE)
        )
    curve_out[...] = column[...].T[:8, :]


def fourth_kernel(
    row_ref, place_ref, curve_ref, value_ref, direction_ref, norm_ref, weights_ref, asked_ref, table,
    solved_out, send_out, solved,
):
    z = place_ref[0]
    curve = jnp.broadcast_to(curve_ref[:1, :], (TILE, LINE_USERS)).T[:, :1]
    direction = direction_ref[...]
    curve = curve + PENALTY * jnp.sum(direction * direction, axis=1, keepdims=True)
    step = norm_ref[:, :1] / curve
    solved[...] = value_ref[...] + step * direction
    solved_out[...] = solved[pl.ds(pl.multiple_of(z * USERS, USERS), USERS), :]
    for j in range(PLANE):
        send_out[j, 3 * LINE_USERS :, :] = jnp.broadcast_to(
            asked_ref[j : j + 1, :], (EXTRA, TILE)
        ).astype(BF)
    for s in range(NZ):
        rows = pl.ds(s * USERS, USERS)
        block = tiles_of(row_ref, table, s)
        weights = weights_ref[rows, :].astype(F32)
        confidence = (1.0 + weights).astype(BF).astype(F32)
        rounded = solved[rows, :].astype(BF)
        coeffs = confidence - weights * against(rounded, block)
        coeffs = jnp.where(weights > 0.0, coeffs, 0.0).astype(BF)
        for j in range(PLANE):
            send_out[j, rows, :] = coeffs[:, j * TILE : (j + 1) * TILE]
            for part in range(2):
                to = pl.ds((1 + part) * LINE_USERS + s * USERS, USERS)
                send_out[j, to, :] = rounded[:, part * TILE : (part + 1) * TILE]


def owner_kernel(got_ref, out_ref, coeffs, rounded):
    for p in range(PLANE):
        users = slice(p * LINE_USERS, (p + 1) * LINE_USERS)
        coeffs[:, users] = got_ref[p, :LINE_USERS, :].astype(F32).T
        rounded[users, :TILE] = got_ref[p, LINE_USERS : 2 * LINE_USERS, :]
        rounded[users, TILE:] = got_ref[p, 2 * LINE_USERS : 3 * LINE_USERS, :]
    asked = jnp.concatenate(
        [got_ref[p, 3 * LINE_USERS :, :].astype(F32)[:1] for p in range(PLANE)], axis=1
    )
    for t in range(out_ref.shape[0] // TILE):
        picked = jnp.where(asked == float(t), coeffs[...], 0.0).astype(BF)
        out_ref[t * TILE : (t + 1) * TILE, :] = jnp.dot(
            picked, rounded[...], preferred_element_type=F32
        )


def call(kernel, outs, operands, spaces, out_spaces, scratch, prefetch=0):
    memory = {"v": pltpu.VMEM, "a": pl.ANY}
    return pl.pallas_call(
        kernel,
        out_shape=outs,
        grid_spec=pltpu.PrefetchScalarGridSpec(
            num_scalar_prefetch=prefetch,
            grid=(1,),
            in_specs=[spec(memory[m]) for m in spaces],
            out_specs=[spec(memory[m]) for m in out_spaces],
            scratch_shapes=scratch,
        ),
        compiler_params=pltpu.CompilerParams(vmem_limit_bytes=VMEM_LIMIT),
    )(*operands)


def spec(space):
    return pl.BlockSpec(memory_space=space)


def shards(item_factors, user_factors, strengths, requests, user_slots):
    z, x, y, c = (lax.axis_index(name) for name in EVERY)
    shape = jax.ShapeDtypeStruct
    pay = jnp.concatenate(
        [
            strengths,
            user_factors,
            jnp.pad(user_slots, ((0, 0), (0, TILE - SLOTS))).astype(BF),
            jnp.broadcast_to(requests, (USERS, TILE)).astype(BF),
        ],
        axis=1,
    )
    half_rows = item_factors.shape[0] // 2
    half = lax.dynamic_slice_in_dim(item_factors, c * half_rows, half_rows, 0)
    half, pay = lax.optimization_barrier((half, pay))
    near = [half] + [lax.ppermute(half, EVERY, ring_pairs(d, 0)) for d in (1, -1, 2)]
    near_a, near_b = jnp.concatenate(near[:2], axis=0), jnp.concatenate(near[2:], axis=0)

    def grow(value, k):
        return jnp.concatenate([value, line_permute(value, lambda s: s ^ k)], axis=0)

    first_two = grow(pay[None], 6)
    held = grow(first_two, 2)
    got = line_permute(held, lambda s: s ^ 1)
    block = shape((BLOCK_ROWS, RANK), BF)
    square = shape((RANK, RANK), F32)
    up_a = lax.ppermute(near_a, EVERY, ring_pairs(1, 1))
    down_b = lax.ppermute(near_b, EVERY, ring_pairs(-1, 1))
    near_a, near_b, gram = call(
        near_kernel, [block, block, square], [near_a, near_b, first_two], "vva", "vvv", []
    )
    up_b = lax.ppermute(near_b, EVERY, ring_pairs(1, 1))
    down_a = lax.ppermute(near_a, EVERY, ring_pairs(-1, 1))
    far_a = lax.ppermute(up_a, EVERY, ring_pairs(1, 1))
    far_b = lax.ppermute(down_b, EVERY, ring_pairs(-1, 1))
    [rest] = call(
        rest_kernel,
        [shape((6 * BLOCK_ROWS, RANK), BF)],
        [up_a, up_b, down_a, down_b, far_a, far_b, got],
        "a" * 7,
        "v",
        [pltpu.SemaphoreType.DMA((6,))],
    )
    [gram_a] = call(gram_kernel, [square], [gram, rest], "vv", "v", [])
    own = [near_a, near_b, rest]
    other = [swap_cores(v) for v in own]
    gram_b = swap_cores(gram_a)
    place = z[None].astype(jnp.int32)
    vectors = shape((LINE_USERS, RANK), F32)
    halves = shape((HALF, RANK), F32)
    weights, start, asked, asked_rows = call(
        weights_kernel,
        [
            shape((LINE_USERS, PLANE_ITEMS), BF),
            vectors,
            shape((NZ, TILE), F32),
            shape((PLANE, LINE_USERS), F32),
        ],
        [place, held, got],
        "vv",
        "vvvv",
        [pltpu.VMEM((LINE_USERS, TILE), F32)],
        prefetch=1,
    )
    asked = lax.dynamic_slice(asked, (0, z * PLANE), (NZ, PLANE))
    tile = jnp.maximum(asked.astype(jnp.int32), 0)
    part_of = tile // 4
    j = jnp.arange(PLANE, dtype=jnp.int32)[None, :]
    along_x = (j // NY - x) % NX
    along_y = (j % NY - y) % NY
    first = jnp.where(part_of == 0, along_y, along_x)
    second = jnp.where(part_of == 0, along_x, along_y)

    def slot(delta):
        return jnp.where(delta == 3, 1, jnp.where(delta == 0, 0, delta + 1))

    first, second = slot(first), slot(second)
    row = jnp.where(part_of == c, 0, 64) + second * 16 + first * 4 + tile % 4
    row = row.reshape(-1)
    part = pltpu.VMEM(vectors.shape, F32)
    keep, give, gram, table = call(
        first_kernel,
        [halves, halves, shape((RANK, RANK), F32), shape((16 * BLOCK_ROWS, RANK), BF)],
        [row, place, start, weights, gram_a, gram_b, *own, *other],
        "vvvv" + "a" * BLOCKS,
        "vvvv",
        [part, pltpu.SemaphoreType.DMA((BLOCKS,))],
        prefetch=2,
    )
    residual, keep, give = call(
        second_kernel,
        [vectors, halves, halves],
        [row, place, *line_sum(keep, give), start, gram, weights, table],
        "v" * 6,
        "vvv",
        [part],
        prefetch=2,
    )
    value, direction, norm, curve = call(
        third_kernel,
        [vectors, vectors, shape((LINE_USERS, TILE), F32), shape((8, LINE_USERS), F32)],
        [row, place, *line_sum(keep, give), start, residual, gram, weights, table],
        "v" * 7,
        "vvvv",
        [part, pltpu.VMEM((LINE_USERS, TILE), F32)],
        prefetch=2,
    )
    for k in (1, 2, 6):
        curve = curve + line_permute(curve, lambda s: s ^ k)
    solved, send = call(
        fourth_kernel,
        [shape((USERS, RANK), F32), shape((PLANE, SEND_ROWS, TILE), BF)],
        [row, place, curve, value, direction, norm, weights, asked_rows, table],
        "v" * 7,
        "vv",
        [part],
        prefetch=2,
    )
    got = lax.all_to_all(send, ("x", "y"), split_axis=0, concat_axis=0, tiled=True)
    [sums] = call(
        owner_kernel,
        [shape(item_factors.shape, F32)],
        [got],
        "v",
        "v",
        [
            pltpu.VMEM((TILE, PLANE * LINE_USERS), F32),
            pltpu.VMEM((PLANE * LINE_USERS, RANK), BF),
        ],
    )
    return solved, sums + swap_cores(sums)


def solution(mesh):
    cut = Mesh(mesh.devices.reshape(NZ, NX, NY, 2), EVERY)
    every, owner = P(EVERY, None), P(("z", "x", "y"), None)
    return jax.shard_map(
        shards,
        mesh=cut,
        in_specs=(owner, every, every, every, every),
        out_specs=(every, owner),
        check_vma=False,
    )
```

```python
import functools

import jax
import jax.numpy as jnp
from jax import lax
from jax.experimental import pallas as pl
from jax.experimental.pallas import tpu as pltpu
from jax.sharding import Mesh, PartitionSpec as P

TILE = 128
RANK = 256
USERS = 16
SLOTS = 8
NZ, NX, NY = 8, 4, 4
PLANE = NX * NY
LINE_USERS = NZ * USERS
PLANE_ITEMS = PLANE * TILE
PENALTY = 1.0
EVERY = ("z", "x", "y", "c")
BF, F32 = jnp.bfloat16, jnp.float32
HIGH = lax.Precision.HIGHEST
WIDE = SLOTS * TILE + RANK + 2 * TILE
EXTRA = 16
VMEM_LIMIT = 16 * 2**20
HALF = LINE_USERS // 2
BLOCKS, BLOCK_ROWS = 6, 1024
SEND_ROWS = 3 * LINE_USERS + EXTRA


def ring_pairs(distance, phase):
    pairs = []
    for z in range(NZ):
        for x in range(NX):
            for y in range(NY):
                for c in range(2):
                    along_y = (c == 0) == (phase == 0)
                    x2 = x if along_y else (x + distance) % NX
                    y2 = (y + distance) % NY if along_y else y
                    pairs.append((((z * NX + x) * NY + y) * 2 + c, ((z * NX + x2) * NY + y2) * 2 + c))
    return pairs


def line_permute(value, partner):
    return lax.ppermute(value, "z", [(s, partner(s)) for s in range(NZ)])


def line_sum(keep, give):
    mine = keep + line_permute(give, lambda s: s ^ 1)
    others = [line_permute(mine, lambda s: (s + k) % NZ) for k in (2, 4, 6)]
    total = mine + others[0] + others[1] + others[2]
    return total, line_permute(total, lambda s: s ^ 1)


def split_halves(place_ref, part, keep_out, give_out):
    side = lax.rem(place_ref[0], 2)
    keep_out[...] = part[pl.ds(pl.multiple_of(side * HALF, HALF), HALF), :]
    give_out[...] = part[pl.ds(pl.multiple_of((1 - side) * HALF, HALF), HALF), :]


def join_halves(place_ref, mine_ref, other_ref, part):
    side = lax.rem(place_ref[0], 2)
    part[pl.ds(pl.multiple_of(side * HALF, HALF), HALF), :] = mine_ref[...]
    part[pl.ds(pl.multiple_of((1 - side) * HALF, HALF), HALF), :] = other_ref[...]


def swap_cores(value):
    return lax.ppermute(value, "c", [(0, 1), (1, 0)])


def against(vectors, block):
    return lax.dot_general(vectors, block, (((1,), (1,)), ((), ())), preferred_element_type=F32)


def tiles_of(row_ref, table, s):
    return jnp.concatenate(
        [
            table[pl.ds(pl.multiple_of(row_ref[s * PLANE + j] * TILE, TILE), TILE), :]
            for j in range(PLANE)
        ],
        axis=0,
    )


def weights_kernel(place_ref, held_ref, got_ref, weights_out, start_out, asked_out, lanes_out, wide):
    z = place_ref[0]
    for s in range(NZ):
        gap = lax.bitwise_xor(z, s)
        pair = lax.div(gap, 2)
        place = jnp.where(pair == 3, 1, jnp.where(pair == 0, 0, pair + 1))
        near = lax.bitwise_and(gap, 1) == 0

        def pay(start, stop):
            held = held_ref[place, :, start:stop].astype(F32)
            return jnp.where(near, held, got_ref[place, :, start:stop].astype(F32))

        rows = pl.ds(s * USERS, USERS)
        start_out[rows, :] = pay(SLOTS * TILE, SLOTS * TILE + RANK)
        slots = pay(SLOTS * TILE + RANK, SLOTS * TILE + RANK + TILE)
        asked = pay(WIDE - TILE, WIDE)
        asked_out[s : s + 1, :] = asked[:1]
        wide[rows, :] = asked
        owners = [jnp.broadcast_to(slots[:, k : k + 1], (USERS, TILE)) for k in range(SLOTS)]
        values = [pay(k * TILE, (k + 1) * TILE) for k in range(SLOTS)]
        for j in range(PLANE):
            owner = (z * PLANE + j).astype(F32)
            total = jnp.zeros((USERS, TILE), F32)
            for k in range(SLOTS):
                total = jnp.where(owners[k] == owner, values[k], total)
            weights_out[rows, j * TILE : (j + 1) * TILE] = total.astype(BF)
    wide[...] = wide[...].T
    lanes_out[...] = wide[pl.ds(pl.multiple_of(z * PLANE, PLANE), PLANE), :]


def gram_of(block):
    return lax.dot_general(block, block, (((0,), (0,)), ((), ())), preferred_element_type=F32)


def near_kernel(near_a, near_b, after_ref, later_a, later_b, gram_out):
    later_a[...] = near_a[...]
    later_b[...] = near_b[...]
    gram_out[...] = gram_of(near_a[...]) + gram_of(near_b[...])


def rest_kernel(*refs):
    sources, (after_ref, table, sems) = refs[:6], refs[6:]
    copies = [
        pltpu.make_async_copy(
            sources[i], table.at[pl.ds(i * BLOCK_ROWS, BLOCK_ROWS)], sems.at[i]
        )
        for i in range(6)
    ]
    for copy in copies:
        copy.start()
    for copy in copies:
        copy.wait()


def gram_kernel(gram_ref, table, gram_out):
    gram = gram_ref[...]
    for i in range(table.shape[0] // BLOCK_ROWS):
        gram = gram + gram_of(table[i * BLOCK_ROWS : (i + 1) * BLOCK_ROWS, :])
    gram_out[...] = gram


def first_kernel(row_ref, place_ref, start_ref, weights_ref, gram_a, gram_b, *rest):
    sources = rest[:BLOCKS]
    keep_out, give_out, gram_out, table, part, sems = rest[BLOCKS:]
    copies, row = [], 0
    for i, source in enumerate(sources):
        to = table.at[pl.ds(row, source.shape[0])]
        copies.append(pltpu.make_async_copy(source, to, sems.at[i]))
        row += source.shape[0]
    for copy in copies:
        copy.start()
    gram = gram_a[...] + gram_b[...]
    gram_out[...] = gram
    part[...] = -jnp.dot(start_ref[...], gram, precision=HIGH, preferred_element_type=F32)
    for copy in copies:
        copy.wait()
    for s in range(NZ):
        rows = pl.ds(s * USERS, USERS)
        block = tiles_of(row_ref, table, s)
        weights = weights_ref[rows, :].astype(F32)
        confidence = jnp.where(weights > 0.0, 1.0 + weights, 0.0).astype(BF)
        scaled = (weights * against(start_ref[rows, :].astype(BF), block)).astype(BF)
        both = jnp.dot(
            jnp.concatenate([confidence, scaled], axis=0), block, preferred_element_type=F32
        )
        part[rows, :] += both[:USERS] - both[USERS:]
    split_halves(place_ref, part, keep_out, give_out)


def second_kernel(
    row_ref, place_ref, mine_ref, other_ref, start_ref, gram_ref, weights_ref, table,
    residual_out, keep_out, give_out, part,
):
    join_halves(place_ref, mine_ref, other_ref, residual_out)
    residual = residual_out[...] - PENALTY * start_ref[...]
    residual_out[...] = residual
    part[...] = jnp.dot(residual, gram_ref[...], precision=HIGH, preferred_element_type=F32)
    for s in range(NZ):
        rows = pl.ds(s * USERS, USERS)
        block = tiles_of(row_ref, table, s)
        weights = weights_ref[rows, :].astype(F32)
        scaled = (weights * against(residual_out[rows, :].astype(BF), block)).astype(BF)
        part[rows, :] += jnp.dot(scaled, block, preferred_element_type=F32)
    split_halves(place_ref, part, keep_out, give_out)


def third_kernel(
    row_ref, place_ref, mine_ref, other_ref, start_ref, residual_ref, gram_ref, weights_ref, table,
    value_out, direction_out, norm_out, curve_out, part, column,
):
    join_halves(place_ref, mine_ref, other_ref, part)
    direction = residual_ref[...]
    image = part[...] + PENALTY * direction
    norm_now = jnp.sum(direction * direction, axis=1, keepdims=True)
    step = norm_now / jnp.sum(direction * image, axis=1, keepdims=True)
    value_out[...] = start_ref[...] + step * direction
    residual = direction - step * image
    norm_next = jnp.sum(residual * residual, axis=1, keepdims=True)
    direction = residual + (norm_next / norm_now) * direction
    direction_out[...] = direction
    norm_out[...] = jnp.broadcast_to(norm_next, (LINE_USERS, TILE))
    image = jnp.dot(direction, gram_ref[...], precision=HIGH, preferred_element_type=F32)
    column[...] = jnp.broadcast_to(
        jnp.sum(direction * image, axis=1, keepdims=True), (LINE_USERS, TILE)
    )
    for s in range(NZ):
        rows = pl.ds(s * USERS, USERS)
        block = tiles_of(row_ref, table, s)
        weights = weights_ref[rows, :].astype(F32)
        fitted = against(direction_out[rows, :].astype(BF), block)
        scaled = (weights * fitted).astype(BF).astype(F32)
        column[rows, :] += jnp.broadcast_to(
            jnp.sum(scaled * fitted, axis=1, keepdims=True), (USERS, TILE)
        )
    curve_out[...] = column[...].T[:8, :]


def fourth_kernel(
    row_ref, place_ref, curve_ref, value_ref, direction_ref, norm_ref, weights_ref, asked_ref, table,
    solved_out, send_out, solved,
):
    z = place_ref[0]
    curve = jnp.broadcast_to(curve_ref[:1, :], (TILE, LINE_USERS)).T[:, :1]
    direction = direction_ref[...]
    curve = curve + PENALTY * jnp.sum(direction * direction, axis=1, keepdims=True)
    step = norm_ref[:, :1] / curve
    solved[...] = value_ref[...] + step * direction
    solved_out[...] = solved[pl.ds(pl.multiple_of(z * USERS, USERS), USERS), :]
    for j in range(PLANE):
        send_out[j, 3 * LINE_USERS :, :] = jnp.broadcast_to(
            asked_ref[j : j + 1, :], (EXTRA, TILE)
        ).astype(BF)
    for s in range(NZ):
        rows = pl.ds(s * USERS, USERS)
        block = tiles_of(row_ref, table, s)
        weights = weights_ref[rows, :].astype(F32)
        confidence = (1.0 + weights).astype(BF).astype(F32)
        rounded = solved[rows, :].astype(BF)
        coeffs = confidence - weights * against(rounded, block)
        coeffs = jnp.where(weights > 0.0, coeffs, 0.0).astype(BF)
        for j in range(PLANE):
            send_out[j, rows, :] = coeffs[:, j * TILE : (j + 1) * TILE]
            for part in range(2):
                to = pl.ds((1 + part) * LINE_USERS + s * USERS, USERS)
                send_out[j, to, :] = rounded[:, part * TILE : (part + 1) * TILE]


def owner_kernel(got_ref, out_ref, coeffs, rounded):
    for p in range(PLANE):
        users = slice(p * LINE_USERS, (p + 1) * LINE_USERS)
        coeffs[:, users] = got_ref[p, :LINE_USERS, :].astype(F32).T
        rounded[users, :TILE] = got_ref[p, LINE_USERS : 2 * LINE_USERS, :]
        rounded[users, TILE:] = got_ref[p, 2 * LINE_USERS : 3 * LINE_USERS, :]
    asked = jnp.concatenate(
        [got_ref[p, 3 * LINE_USERS :, :].astype(F32)[:1] for p in range(PLANE)], axis=1
    )
    for t in range(out_ref.shape[0] // TILE):
        picked = jnp.where(asked == float(t), coeffs[...], 0.0).astype(BF)
        out_ref[t * TILE : (t + 1) * TILE, :] = jnp.dot(
            picked, rounded[...], preferred_element_type=F32
        )


def call(kernel, outs, operands, spaces, out_spaces, scratch, prefetch=0):
    memory = {"v": pltpu.VMEM, "a": pl.ANY}
    return pl.pallas_call(
        kernel,
        out_shape=outs,
        grid_spec=pltpu.PrefetchScalarGridSpec(
            num_scalar_prefetch=prefetch,
            grid=(1,),
            in_specs=[spec(memory[m]) for m in spaces],
            out_specs=[spec(memory[m]) for m in out_spaces],
            scratch_shapes=scratch,
        ),
        compiler_params=pltpu.CompilerParams(vmem_limit_bytes=VMEM_LIMIT),
    )(*operands)


def spec(space):
    return pl.BlockSpec(memory_space=space)


def shards(item_factors, user_factors, strengths, requests, user_slots):
    z, x, y, c = (lax.axis_index(name) for name in EVERY)
    shape = jax.ShapeDtypeStruct
    pay = jnp.concatenate(
        [
            strengths,
            user_factors,
            jnp.pad(user_slots, ((0, 0), (0, TILE - SLOTS))).astype(BF),
            jnp.broadcast_to(requests, (USERS, TILE)).astype(BF),
        ],
        axis=1,
    )
    half_rows = item_factors.shape[0] // 2
    half = lax.dynamic_slice_in_dim(item_factors, c * half_rows, half_rows, 0)
    near = [half] + [lax.ppermute(half, EVERY, ring_pairs(d, 0)) for d in (1, -1, 2)]
    near_a, near_b = jnp.concatenate(near[:2], axis=0), jnp.concatenate(near[2:], axis=0)

    def grow(value, k):
        return jnp.concatenate([value, line_permute(value, lambda s: s ^ k)], axis=0)

    first_two = grow(pay[None], 6)
    held = grow(first_two, 2)
    got = line_permute(held, lambda s: s ^ 1)
    block = shape((BLOCK_ROWS, RANK), BF)
    square = shape((RANK, RANK), F32)
    up_a = lax.ppermute(near_a, EVERY, ring_pairs(1, 1))
    down_b = lax.ppermute(near_b, EVERY, ring_pairs(-1, 1))
    near_a, near_b, gram = call(
        near_kernel, [block, block, square], [near_a, near_b, first_two], "vva", "vvv", []
    )
    up_b = lax.ppermute(near_b, EVERY, ring_pairs(1, 1))
    down_a = lax.ppermute(near_a, EVERY, ring_pairs(-1, 1))
    far_a = lax.ppermute(up_a, EVERY, ring_pairs(1, 1))
    far_b = lax.ppermute(down_b, EVERY, ring_pairs(-1, 1))
    [rest] = call(
        rest_kernel,
        [shape((6 * BLOCK_ROWS, RANK), BF)],
        [up_a, up_b, down_a, down_b, far_a, far_b, got],
        "a" * 7,
        "v",
        [pltpu.SemaphoreType.DMA((6,))],
    )
    [gram_a] = call(gram_kernel, [square], [gram, rest], "vv", "v", [])
    own = [near_a, near_b, rest]
    other = [swap_cores(v) for v in own]
    gram_b = swap_cores(gram_a)
    place = z[None].astype(jnp.int32)
    vectors = shape((LINE_USERS, RANK), F32)
    halves = shape((HALF, RANK), F32)
    weights, start, asked, asked_rows = call(
        weights_kernel,
        [
            shape((LINE_USERS, PLANE_ITEMS), BF),
            vectors,
            shape((NZ, TILE), F32),
            shape((PLANE, LINE_USERS), F32),
        ],
        [place, held, got],
        "vv",
        "vvvv",
        [pltpu.VMEM((LINE_USERS, TILE), F32)],
        prefetch=1,
    )
    asked = lax.dynamic_slice(asked, (0, z * PLANE), (NZ, PLANE))
    tile = jnp.maximum(asked.astype(jnp.int32), 0)
    part_of = tile // 4
    j = jnp.arange(PLANE, dtype=jnp.int32)[None, :]
    along_x = (j // NY - x) % NX
    along_y = (j % NY - y) % NY
    first = jnp.where(part_of == 0, along_y, along_x)
    second = jnp.where(part_of == 0, along_x, along_y)

    def slot(delta):
        return jnp.where(delta == 3, 1, jnp.where(delta == 0, 0, delta + 1))

    first, second = slot(first), slot(second)
    row = jnp.where(part_of == c, 0, 64) + second * 16 + first * 4 + tile % 4
    row = row.reshape(-1)
    part = pltpu.VMEM(vectors.shape, F32)
    keep, give, gram, table = call(
        first_kernel,
        [halves, halves, shape((RANK, RANK), F32), shape((16 * BLOCK_ROWS, RANK), BF)],
        [row, place, start, weights, gram_a, gram_b, *own, *other],
        "vvvv" + "a" * BLOCKS,
        "vvvv",
        [part, pltpu.SemaphoreType.DMA((BLOCKS,))],
        prefetch=2,
    )
    residual, keep, give = call(
        second_kernel,
        [vectors, halves, halves],
        [row, place, *line_sum(keep, give), start, gram, weights, table],
        "v" * 6,
        "vvv",
        [part],
        prefetch=2,
    )
    value, direction, norm, curve = call(
        third_kernel,
        [vectors, vectors, shape((LINE_USERS, TILE), F32), shape((8, LINE_USERS), F32)],
        [row, place, *line_sum(keep, give), start, residual, gram, weights, table],
        "v" * 7,
        "vvvv",
        [part, pltpu.VMEM((LINE_USERS, TILE), F32)],
        prefetch=2,
    )
    for k in (1, 2, 6):
        curve = curve + line_permute(curve, lambda s: s ^ k)
    solved, send = call(
        fourth_kernel,
        [shape((USERS, RANK), F32), shape((PLANE, SEND_ROWS, TILE), BF)],
        [row, place, curve, value, direction, norm, weights, asked_rows, table],
        "v" * 7,
        "vv",
        [part],
        prefetch=2,
    )
    got = lax.all_to_all(send, ("x", "y"), split_axis=0, concat_axis=0, tiled=True)
    [sums] = call(
        owner_kernel,
        [shape(item_factors.shape, F32)],
        [got],
        "v",
        "v",
        [
            pltpu.VMEM((TILE, PLANE * LINE_USERS), F32),
            pltpu.VMEM((PLANE * LINE_USERS, RANK), BF),
        ],
    )
    return solved, sums + swap_cores(sums)


def solution(mesh):
    cut = Mesh(mesh.devices.reshape(NZ, NX, NY, 2), EVERY)
    every, owner = P(EVERY, None), P(("z", "x", "y"), None)
    return jax.shard_map(
        shards,
        mesh=cut,
        in_specs=(owner, every, every, every, every),
        out_specs=(every, owner),
        check_vma=False,
    )
```

```python
import functools

import jax
import jax.numpy as jnp
from jax import lax
from jax.experimental import pallas as pl
from jax.experimental.pallas import tpu as pltpu
from jax.sharding import Mesh, PartitionSpec as P

TILE = 128
RANK = 256
USERS = 16
SLOTS = 8
NZ, NX, NY = 8, 4, 4
PLANE = NX * NY
LINE_USERS = NZ * USERS
PLANE_ITEMS = PLANE * TILE
PENALTY = 1.0
EVERY = ("z", "x", "y", "c")
BF, F32 = jnp.bfloat16, jnp.float32
HIGH = lax.Precision.HIGHEST
WIDE = SLOTS * TILE + RANK + 2 * TILE
EXTRA = 16
VMEM_LIMIT = 16 * 2**20
HALF = LINE_USERS // 2
BLOCKS, BLOCK_ROWS = 6, 1024
SEND_ROWS = 3 * LINE_USERS + EXTRA


def ring_pairs(distance, phase):
    pairs = []
    for z in range(NZ):
        for x in range(NX):
            for y in range(NY):
                for c in range(2):
                    along_y = (c == 0) == (phase == 0)
                    x2 = x if along_y else (x + distance) % NX
                    y2 = (y + distance) % NY if along_y else y
                    pairs.append((((z * NX + x) * NY + y) * 2 + c, ((z * NX + x2) * NY + y2) * 2 + c))
    return pairs


def line_permute(value, partner):
    return lax.ppermute(value, "z", [(s, partner(s)) for s in range(NZ)])


def line_sum(keep, give):
    mine = keep + line_permute(give, lambda s: s ^ 1)
    others = [line_permute(mine, lambda s: (s + k) % NZ) for k in (2, 4, 6)]
    total = mine + others[0] + others[1] + others[2]
    return total, line_permute(total, lambda s: s ^ 1)


def split_halves(place_ref, part, keep_out, give_out):
    side = lax.rem(place_ref[0], 2)
    keep_out[...] = part[pl.ds(pl.multiple_of(side * HALF, HALF), HALF), :]
    give_out[...] = part[pl.ds(pl.multiple_of((1 - side) * HALF, HALF), HALF), :]


def join_halves(place_ref, mine_ref, other_ref, part):
    side = lax.rem(place_ref[0], 2)
    part[pl.ds(pl.multiple_of(side * HALF, HALF), HALF), :] = mine_ref[...]
    part[pl.ds(pl.multiple_of((1 - side) * HALF, HALF), HALF), :] = other_ref[...]


def swap_cores(value):
    return lax.ppermute(value, "c", [(0, 1), (1, 0)])


def against(vectors, block):
    return lax.dot_general(vectors, block, (((1,), (1,)), ((), ())), preferred_element_type=F32)


def tiles_of(row_ref, table, s):
    return jnp.concatenate(
        [
            table[pl.ds(pl.multiple_of(row_ref[s * PLANE + j] * TILE, TILE), TILE), :]
            for j in range(PLANE)
        ],
        axis=0,
    )


def weights_kernel(place_ref, held_ref, got_ref, weights_out, start_out, asked_out, lanes_out, wide):
    z = place_ref[0]
    for s in range(NZ):
        gap = lax.bitwise_xor(z, s)
        pair = lax.div(gap, 2)
        place = jnp.where(pair == 3, 1, jnp.where(pair == 0, 0, pair + 1))
        near = lax.bitwise_and(gap, 1) == 0

        def pay(start, stop):
            held = held_ref[place, :, start:stop].astype(F32)
            return jnp.where(near, held, got_ref[place, :, start:stop].astype(F32))

        rows = pl.ds(s * USERS, USERS)
        start_out[rows, :] = pay(SLOTS * TILE, SLOTS * TILE + RANK)
        slots = pay(SLOTS * TILE + RANK, SLOTS * TILE + RANK + TILE)
        asked = pay(WIDE - TILE, WIDE)
        asked_out[s : s + 1, :] = asked[:1]
        wide[rows, :] = asked
        owners = [jnp.broadcast_to(slots[:, k : k + 1], (USERS, TILE)) for k in range(SLOTS)]
        values = [pay(k * TILE, (k + 1) * TILE) for k in range(SLOTS)]
        for j in range(PLANE):
            owner = (z * PLANE + j).astype(F32)
            total = jnp.zeros((USERS, TILE), F32)
            for k in range(SLOTS):
                total = jnp.where(owners[k] == owner, values[k], total)
            weights_out[rows, j * TILE : (j + 1) * TILE] = total.astype(BF)
    wide[...] = wide[...].T
    lanes_out[...] = wide[pl.ds(pl.multiple_of(z * PLANE, PLANE), PLANE), :]


def gram_of(block):
    return lax.dot_general(block, block, (((0,), (0,)), ((), ())), preferred_element_type=F32)


def join_kernel(one, two, three, four, after_ref, near_a, near_b, gram_out):
    rows = one.shape[0]
    near_a[:rows, :] = one[...]
    near_a[rows:, :] = two[...]
    near_b[:rows, :] = three[...]
    near_b[rows:, :] = four[...]
    gram = gram_of(one[...])
    for block in (two, three, four):
        gram = gram + gram_of(block[...])
    gram_out[...] = gram


def rest_kernel(*refs):
    sources, (after_ref, table, sems) = refs[:6], refs[6:]
    copies = [
        pltpu.make_async_copy(
            sources[i], table.at[pl.ds(i * BLOCK_ROWS, BLOCK_ROWS)], sems.at[i]
        )
        for i in range(6)
    ]
    for copy in copies:
        copy.start()
    for copy in copies:
        copy.wait()


def gram_kernel(gram_ref, table, gram_out):
    gram = gram_ref[...]
    for i in range(table.shape[0] // BLOCK_ROWS):
        gram = gram + gram_of(table[i * BLOCK_ROWS : (i + 1) * BLOCK_ROWS, :])
    gram_out[...] = gram


def first_kernel(row_ref, place_ref, start_ref, weights_ref, gram_a, gram_b, *rest):
    sources = rest[:BLOCKS]
    keep_out, give_out, gram_out, table, part, sems = rest[BLOCKS:]
    copies, row = [], 0
    for i, source in enumerate(sources):
        to = table.at[pl.ds(row, source.shape[0])]
        copies.append(pltpu.make_async_copy(source, to, sems.at[i]))
        row += source.shape[0]
    for copy in copies:
        copy.start()
    gram = gram_a[...] + gram_b[...]
    gram_out[...] = gram
    part[...] = -jnp.dot(start_ref[...], gram, precision=HIGH, preferred_element_type=F32)
    for copy in copies:
        copy.wait()
    for s in range(NZ):
        rows = pl.ds(s * USERS, USERS)
        block = tiles_of(row_ref, table, s)
        weights = weights_ref[rows, :].astype(F32)
        confidence = jnp.where(weights > 0.0, 1.0 + weights, 0.0).astype(BF)
        scaled = (weights * against(start_ref[rows, :].astype(BF), block)).astype(BF)
        both = jnp.dot(
            jnp.concatenate([confidence, scaled], axis=0), block, preferred_element_type=F32
        )
        part[rows, :] += both[:USERS] - both[USERS:]
    split_halves(place_ref, part, keep_out, give_out)


def second_kernel(
    row_ref, place_ref, mine_ref, other_ref, start_ref, gram_ref, weights_ref, table,
    residual_out, keep_out, give_out, part,
):
    join_halves(place_ref, mine_ref, other_ref, residual_out)
    residual = residual_out[...] - PENALTY * start_ref[...]
    residual_out[...] = residual
    part[...] = jnp.dot(residual, gram_ref[...], precision=HIGH, preferred_element_type=F32)
    for s in range(NZ):
        rows = pl.ds(s * USERS, USERS)
        block = tiles_of(row_ref, table, s)
        weights = weights_ref[rows, :].astype(F32)
        scaled = (weights * against(residual_out[rows, :].astype(BF), block)).astype(BF)
        part[rows, :] += jnp.dot(scaled, block, preferred_element_type=F32)
    split_halves(place_ref, part, keep_out, give_out)


def third_kernel(
    row_ref, place_ref, mine_ref, other_ref, start_ref, residual_ref, gram_ref, weights_ref, table,
    value_out, direction_out, norm_out, curve_out, part, column,
):
    join_halves(place_ref, mine_ref, other_ref, part)
    direction = residual_ref[...]
    image = part[...] + PENALTY * direction
    norm_now = jnp.sum(direction * direction, axis=1, keepdims=True)
    step = norm_now / jnp.sum(direction * image, axis=1, keepdims=True)
    value_out[...] = start_ref[...] + step * direction
    residual = direction - step * image
    norm_next = jnp.sum(residual * residual, axis=1, keepdims=True)
    direction = residual + (norm_next / norm_now) * direction
    direction_out[...] = direction
    norm_out[...] = jnp.broadcast_to(norm_next, (LINE_USERS, TILE))
    image = jnp.dot(direction, gram_ref[...], precision=HIGH, preferred_element_type=F32)
    column[...] = jnp.broadcast_to(
        jnp.sum(direction * image, axis=1, keepdims=True), (LINE_USERS, TILE)
    )
    for s in range(NZ):
        rows = pl.ds(s * USERS, USERS)
        block = tiles_of(row_ref, table, s)
        weights = weights_ref[rows, :].astype(F32)
        fitted = against(direction_out[rows, :].astype(BF), block)
        scaled = (weights * fitted).astype(BF).astype(F32)
        column[rows, :] += jnp.broadcast_to(
            jnp.sum(scaled * fitted, axis=1, keepdims=True), (USERS, TILE)
        )
    curve_out[...] = column[...].T[:8, :]


def fourth_kernel(
    row_ref, place_ref, curve_ref, value_ref, direction_ref, norm_ref, weights_ref, asked_ref, table,
    solved_out, send_out, solved,
):
    z = place_ref[0]
    curve = jnp.broadcast_to(curve_ref[:1, :], (TILE, LINE_USERS)).T[:, :1]
    direction = direction_ref[...]
    curve = curve + PENALTY * jnp.sum(direction * direction, axis=1, keepdims=True)
    step = norm_ref[:, :1] / curve
    solved[...] = value_ref[...] + step * direction
    solved_out[...] = solved[pl.ds(pl.multiple_of(z * USERS, USERS), USERS), :]
    for j in range(PLANE):
        send_out[j, 3 * LINE_USERS :, :] = jnp.broadcast_to(
            asked_ref[j : j + 1, :], (EXTRA, TILE)
        ).astype(BF)
    for s in range(NZ):
        rows = pl.ds(s * USERS, USERS)
        block = tiles_of(row_ref, table, s)
        weights = weights_ref[rows, :].astype(F32)
        confidence = (1.0 + weights).astype(BF).astype(F32)
        rounded = solved[rows, :].astype(BF)
        coeffs = confidence - weights * against(rounded, block)
        coeffs = jnp.where(weights > 0.0, coeffs, 0.0).astype(BF)
        for j in range(PLANE):
            send_out[j, rows, :] = coeffs[:, j * TILE : (j + 1) * TILE]
            for part in range(2):
                to = pl.ds((1 + part) * LINE_USERS + s * USERS, USERS)
                send_out[j, to, :] = rounded[:, part * TILE : (part + 1) * TILE]


def owner_kernel(got_ref, out_ref, coeffs, rounded):
    for p in range(PLANE):
        users = slice(p * LINE_USERS, (p + 1) * LINE_USERS)
        coeffs[:, users] = got_ref[p, :LINE_USERS, :].astype(F32).T
        rounded[users, :TILE] = got_ref[p, LINE_USERS : 2 * LINE_USERS, :]
        rounded[users, TILE:] = got_ref[p, 2 * LINE_USERS : 3 * LINE_USERS, :]
    asked = jnp.concatenate(
        [got_ref[p, 3 * LINE_USERS :, :].astype(F32)[:1] for p in range(PLANE)], axis=1
    )
    for t in range(out_ref.shape[0] // TILE):
        picked = jnp.where(asked == float(t), coeffs[...], 0.0).astype(BF)
        out_ref[t * TILE : (t + 1) * TILE, :] = jnp.dot(
            picked, rounded[...], preferred_element_type=F32
        )


def call(kernel, outs, operands, spaces, out_spaces, scratch, prefetch=0):
    memory = {"v": pltpu.VMEM, "a": pl.ANY}
    return pl.pallas_call(
        kernel,
        out_shape=outs,
        grid_spec=pltpu.PrefetchScalarGridSpec(
            num_scalar_prefetch=prefetch,
            grid=(1,),
            in_specs=[spec(memory[m]) for m in spaces],
            out_specs=[spec(memory[m]) for m in out_spaces],
            scratch_shapes=scratch,
        ),
        compiler_params=pltpu.CompilerParams(vmem_limit_bytes=VMEM_LIMIT),
    )(*operands)


def spec(space):
    return pl.BlockSpec(memory_space=space)


def shards(item_factors, user_factors, strengths, requests, user_slots):
    z, x, y, c = (lax.axis_index(name) for name in EVERY)
    shape = jax.ShapeDtypeStruct
    pay = jnp.concatenate(
        [
            strengths,
            user_factors,
            jnp.pad(user_slots, ((0, 0), (0, TILE - SLOTS))).astype(BF),
            jnp.broadcast_to(requests, (USERS, TILE)).astype(BF),
        ],
        axis=1,
    )
    half_rows = item_factors.shape[0] // 2
    half = lax.dynamic_slice_in_dim(item_factors, c * half_rows, half_rows, 0)
    near = [half] + [lax.ppermute(half, EVERY, ring_pairs(d, 0)) for d in (1, -1, 2)]

    def grow(value, k):
        return jnp.concatenate([value, line_permute(value, lambda s: s ^ k)], axis=0)

    first_two = grow(pay[None], 6)
    held = grow(first_two, 2)
    got = line_permute(held, lambda s: s ^ 1)
    block = shape((BLOCK_ROWS, RANK), BF)
    square = shape((RANK, RANK), F32)
    near_a, near_b, gram = call(
        join_kernel, [block, block, square], [*near, first_two], "vvvva", "vvv", []
    )
    up_a = lax.ppermute(near_a, EVERY, ring_pairs(1, 1))
    down_b = lax.ppermute(near_b, EVERY, ring_pairs(-1, 1))
    up_b = lax.ppermute(near_b, EVERY, ring_pairs(1, 1))
    down_a = lax.ppermute(near_a, EVERY, ring_pairs(-1, 1))
    far_a = lax.ppermute(up_a, EVERY, ring_pairs(1, 1))
    far_b = lax.ppermute(down_b, EVERY, ring_pairs(-1, 1))
    [rest] = call(
        rest_kernel,
        [shape((6 * BLOCK_ROWS, RANK), BF)],
        [up_a, up_b, down_a, down_b, far_a, far_b, got],
        "a" * 7,
        "v",
        [pltpu.SemaphoreType.DMA((6,))],
    )
    [gram_a] = call(gram_kernel, [square], [gram, rest], "vv", "v", [])
    own = [near_a, near_b, rest]
    other = [swap_cores(v) for v in own]
    gram_b = swap_cores(gram_a)
    place = z[None].astype(jnp.int32)
    vectors = shape((LINE_USERS, RANK), F32)
    halves = shape((HALF, RANK), F32)
    weights, start, asked, asked_rows = call(
        weights_kernel,
        [
            shape((LINE_USERS, PLANE_ITEMS), BF),
            vectors,
            shape((NZ, TILE), F32),
            shape((PLANE, LINE_USERS), F32),
        ],
        [place, held, got],
        "vv",
        "vvvv",
        [pltpu.VMEM((LINE_USERS, TILE), F32)],
        prefetch=1,
    )
    asked = lax.dynamic_slice(asked, (0, z * PLANE), (NZ, PLANE))
    tile = jnp.maximum(asked.astype(jnp.int32), 0)
    part_of = tile // 4
    j = jnp.arange(PLANE, dtype=jnp.int32)[None, :]
    along_x = (j // NY - x) % NX
    along_y = (j % NY - y) % NY
    first = jnp.where(part_of == 0, along_y, along_x)
    second = jnp.where(part_of == 0, along_x, along_y)

    def slot(delta):
        return jnp.where(delta == 3, 1, jnp.where(delta == 0, 0, delta + 1))

    first, second = slot(first), slot(second)
    row = jnp.where(part_of == c, 0, 64) + second * 16 + first * 4 + tile % 4
    row = row.reshape(-1)
    part = pltpu.VMEM(vectors.shape, F32)
    keep, give, gram, table = call(
        first_kernel,
        [halves, halves, shape((RANK, RANK), F32), shape((16 * BLOCK_ROWS, RANK), BF)],
        [row, place, start, weights, gram_a, gram_b, *own, *other],
        "vvvv" + "a" * BLOCKS,
        "vvvv",
        [part, pltpu.SemaphoreType.DMA((BLOCKS,))],
        prefetch=2,
    )
    residual, keep, give = call(
        second_kernel,
        [vectors, halves, halves],
        [row, place, *line_sum(keep, give), start, gram, weights, table],
        "v" * 6,
        "vvv",
        [part],
        prefetch=2,
    )
    value, direction, norm, curve = call(
        third_kernel,
        [vectors, vectors, shape((LINE_USERS, TILE), F32), shape((8, LINE_USERS), F32)],
        [row, place, *line_sum(keep, give), start, residual, gram, weights, table],
        "v" * 7,
        "vvvv",
        [part, pltpu.VMEM((LINE_USERS, TILE), F32)],
        prefetch=2,
    )
    for k in (1, 2, 6):
        curve = curve + line_permute(curve, lambda s: s ^ k)
    solved, send = call(
        fourth_kernel,
        [shape((USERS, RANK), F32), shape((PLANE, SEND_ROWS, TILE), BF)],
        [row, place, curve, value, direction, norm, weights, asked_rows, table],
        "v" * 7,
        "vv",
        [part],
        prefetch=2,
    )
    got = lax.all_to_all(send, ("x", "y"), split_axis=0, concat_axis=0, tiled=True)
    [sums] = call(
        owner_kernel,
        [shape(item_factors.shape, F32)],
        [got],
        "v",
        "v",
        [
            pltpu.VMEM((TILE, PLANE * LINE_USERS), F32),
            pltpu.VMEM((PLANE * LINE_USERS, RANK), BF),
        ],
    )
    return solved, sums + swap_cores(sums)


def solution(mesh):
    cut = Mesh(mesh.devices.reshape(NZ, NX, NY, 2), EVERY)
    every, owner = P(EVERY, None), P(("z", "x", "y"), None)
    return jax.shard_map(
        shards,
        mesh=cut,
        in_specs=(owner, every, every, every, every),
        out_specs=(every, owner),
        check_vma=False,
    )
```

```python
import functools

import jax
import jax.numpy as jnp
from jax import lax
from jax.experimental import pallas as pl
from jax.experimental.pallas import tpu as pltpu
from jax.sharding import Mesh, PartitionSpec as P

TILE = 128
RANK = 256
USERS = 16
SLOTS = 8
NZ, NX, NY = 8, 4, 4
PLANE = NX * NY
LINE_USERS = NZ * USERS
PLANE_ITEMS = PLANE * TILE
PENALTY = 1.0
EVERY = ("z", "x", "y", "c")
BF, F32 = jnp.bfloat16, jnp.float32
HIGH = lax.Precision.HIGHEST
WIDE = SLOTS * TILE + RANK + 2 * TILE
EXTRA = 16
VMEM_LIMIT = 16 * 2**20
HALF = LINE_USERS // 2
BLOCKS, BLOCK_ROWS = 6, 1024
SEND_ROWS = 3 * LINE_USERS + EXTRA


def ring_pairs(distance, phase):
    pairs = []
    for z in range(NZ):
        for x in range(NX):
            for y in range(NY):
                for c in range(2):
                    along_y = (c == 0) == (phase == 0)
                    x2 = x if along_y else (x + distance) % NX
                    y2 = (y + distance) % NY if along_y else y
                    pairs.append((((z * NX + x) * NY + y) * 2 + c, ((z * NX + x2) * NY + y2) * 2 + c))
    return pairs


def line_permute(value, partner):
    return lax.ppermute(value, "z", [(s, partner(s)) for s in range(NZ)])


def line_sum(keep, give):
    mine = keep + line_permute(give, lambda s: s ^ 1)
    others = [line_permute(mine, lambda s: (s + k) % NZ) for k in (2, 4, 6)]
    total = mine + others[0] + others[1] + others[2]
    return total, line_permute(total, lambda s: s ^ 1)


def split_halves(place_ref, part, keep_out, give_out):
    side = lax.rem(place_ref[0], 2)
    keep_out[...] = part[pl.ds(pl.multiple_of(side * HALF, HALF), HALF), :]
    give_out[...] = part[pl.ds(pl.multiple_of((1 - side) * HALF, HALF), HALF), :]


def join_halves(place_ref, mine_ref, other_ref, part):
    side = lax.rem(place_ref[0], 2)
    part[pl.ds(pl.multiple_of(side * HALF, HALF), HALF), :] = mine_ref[...]
    part[pl.ds(pl.multiple_of((1 - side) * HALF, HALF), HALF), :] = other_ref[...]


def swap_cores(value):
    return lax.ppermute(value, "c", [(0, 1), (1, 0)])


def against(vectors, block):
    return lax.dot_general(vectors, block, (((1,), (1,)), ((), ())), preferred_element_type=F32)


def tiles_of(row_ref, table, s):
    return jnp.concatenate(
        [
            table[pl.ds(pl.multiple_of(row_ref[s * PLANE + j] * TILE, TILE), TILE), :]
            for j in range(PLANE)
        ],
        axis=0,
    )


def weights_kernel(place_ref, held_ref, got_ref, weights_out, start_out, asked_out, lanes_out, wide):
    z = place_ref[0]
    for s in range(NZ):
        gap = lax.bitwise_xor(z, s)
        near = gap < 4
        place = jnp.where(near, gap, lax.bitwise_xor(gap, 6))

        def pay(start, stop):
            held = held_ref[place, :, start:stop].astype(F32)
            return jnp.where(near, held, got_ref[place, :, start:stop].astype(F32))

        rows = pl.ds(s * USERS, USERS)
        start_out[rows, :] = pay(SLOTS * TILE, SLOTS * TILE + RANK)
        slots = pay(SLOTS * TILE + RANK, SLOTS * TILE + RANK + TILE)
        asked = pay(WIDE - TILE, WIDE)
        asked_out[s : s + 1, :] = asked[:1]
        wide[rows, :] = asked
        owners = [jnp.broadcast_to(slots[:, k : k + 1], (USERS, TILE)) for k in range(SLOTS)]
        values = [pay(k * TILE, (k + 1) * TILE) for k in range(SLOTS)]
        for j in range(PLANE):
            owner = (z * PLANE + j).astype(F32)
            total = jnp.zeros((USERS, TILE), F32)
            for k in range(SLOTS):
                total = jnp.where(owners[k] == owner, values[k], total)
            weights_out[rows, j * TILE : (j + 1) * TILE] = total.astype(BF)
    wide[...] = wide[...].T
    lanes_out[...] = wide[pl.ds(pl.multiple_of(z * PLANE, PLANE), PLANE), :]


def gram_of(block):
    return lax.dot_general(block, block, (((0,), (0,)), ((), ())), preferred_element_type=F32)


def join_kernel(one, two, three, four, after_ref, near_a, near_b, gram_out):
    rows = one.shape[0]
    near_a[:rows, :] = one[...]
    near_a[rows:, :] = two[...]
    near_b[:rows, :] = three[...]
    near_b[rows:, :] = four[...]
    gram = gram_of(one[...])
    for block in (two, three, four):
        gram = gram + gram_of(block[...])
    gram_out[...] = gram


def rest_kernel(*refs):
    sources, (after_ref, table, sems) = refs[:6], refs[6:]
    copies = [
        pltpu.make_async_copy(
            sources[i], table.at[pl.ds(i * BLOCK_ROWS, BLOCK_ROWS)], sems.at[i]
        )
        for i in range(6)
    ]
    for copy in copies:
        copy.start()
    for copy in copies:
        copy.wait()


def gram_kernel(gram_ref, table, gram_out):
    gram = gram_ref[...]
    for i in range(table.shape[0] // BLOCK_ROWS):
        gram = gram + gram_of(table[i * BLOCK_ROWS : (i + 1) * BLOCK_ROWS, :])
    gram_out[...] = gram


def first_kernel(row_ref, place_ref, start_ref, weights_ref, gram_a, gram_b, *rest):
    sources = rest[:BLOCKS]
    keep_out, give_out, gram_out, table, part, sems = rest[BLOCKS:]
    copies, row = [], 0
    for i, source in enumerate(sources):
        to = table.at[pl.ds(row, source.shape[0])]
        copies.append(pltpu.make_async_copy(source, to, sems.at[i]))
        row += source.shape[0]
    for copy in copies:
        copy.start()
    gram = gram_a[...] + gram_b[...]
    gram_out[...] = gram
    part[...] = -jnp.dot(start_ref[...], gram, precision=HIGH, preferred_element_type=F32)
    for copy in copies:
        copy.wait()
    for s in range(NZ):
        rows = pl.ds(s * USERS, USERS)
        block = tiles_of(row_ref, table, s)
        weights = weights_ref[rows, :].astype(F32)
        confidence = jnp.where(weights > 0.0, 1.0 + weights, 0.0).astype(BF)
        scaled = (weights * against(start_ref[rows, :].astype(BF), block)).astype(BF)
        both = jnp.dot(
            jnp.concatenate([confidence, scaled], axis=0), block, preferred_element_type=F32
        )
        part[rows, :] += both[:USERS] - both[USERS:]
    split_halves(place_ref, part, keep_out, give_out)


def second_kernel(
    row_ref, place_ref, mine_ref, other_ref, start_ref, gram_ref, weights_ref, table,
    residual_out, keep_out, give_out, part,
):
    join_halves(place_ref, mine_ref, other_ref, residual_out)
    residual = residual_out[...] - PENALTY * start_ref[...]
    residual_out[...] = residual
    part[...] = jnp.dot(residual, gram_ref[...], precision=HIGH, preferred_element_type=F32)
    for s in range(NZ):
        rows = pl.ds(s * USERS, USERS)
        block = tiles_of(row_ref, table, s)
        weights = weights_ref[rows, :].astype(F32)
        scaled = (weights * against(residual_out[rows, :].astype(BF), block)).astype(BF)
        part[rows, :] += jnp.dot(scaled, block, preferred_element_type=F32)
    split_halves(place_ref, part, keep_out, give_out)


def third_kernel(
    row_ref, place_ref, mine_ref, other_ref, start_ref, residual_ref, gram_ref, weights_ref, table,
    value_out, direction_out, norm_out, curve_out, part, column,
):
    join_halves(place_ref, mine_ref, other_ref, part)
    direction = residual_ref[...]
    image = part[...] + PENALTY * direction
    norm_now = jnp.sum(direction * direction, axis=1, keepdims=True)
    step = norm_now / jnp.sum(direction * image, axis=1, keepdims=True)
    value_out[...] = start_ref[...] + step * direction
    residual = direction - step * image
    norm_next = jnp.sum(residual * residual, axis=1, keepdims=True)
    direction = residual + (norm_next / norm_now) * direction
    direction_out[...] = direction
    norm_out[...] = jnp.broadcast_to(norm_next, (LINE_USERS, TILE))
    image = jnp.dot(direction, gram_ref[...], precision=HIGH, preferred_element_type=F32)
    column[...] = jnp.broadcast_to(
        jnp.sum(direction * image, axis=1, keepdims=True), (LINE_USERS, TILE)
    )
    for s in range(NZ):
        rows = pl.ds(s * USERS, USERS)
        block = tiles_of(row_ref, table, s)
        weights = weights_ref[rows, :].astype(F32)
        fitted = against(direction_out[rows, :].astype(BF), block)
        scaled = (weights * fitted).astype(BF).astype(F32)
        column[rows, :] += jnp.broadcast_to(
            jnp.sum(scaled * fitted, axis=1, keepdims=True), (USERS, TILE)
        )
    curve_out[...] = column[...].T[:8, :]


def fourth_kernel(
    row_ref, place_ref, curve_ref, value_ref, direction_ref, norm_ref, weights_ref, asked_ref, table,
    solved_out, send_out, solved,
):
    z = place_ref[0]
    curve = jnp.broadcast_to(curve_ref[:1, :], (TILE, LINE_USERS)).T[:, :1]
    direction = direction_ref[...]
    curve = curve + PENALTY * jnp.sum(direction * direction, axis=1, keepdims=True)
    step = norm_ref[:, :1] / curve
    solved[...] = value_ref[...] + step * direction
    solved_out[...] = solved[pl.ds(pl.multiple_of(z * USERS, USERS), USERS), :]
    for j in range(PLANE):
        send_out[j, 3 * LINE_USERS :, :] = jnp.broadcast_to(
            asked_ref[j : j + 1, :], (EXTRA, TILE)
        ).astype(BF)
    for s in range(NZ):
        rows = pl.ds(s * USERS, USERS)
        block = tiles_of(row_ref, table, s)
        weights = weights_ref[rows, :].astype(F32)
        confidence = (1.0 + weights).astype(BF).astype(F32)
        rounded = solved[rows, :].astype(BF)
        coeffs = confidence - weights * against(rounded, block)
        coeffs = jnp.where(weights > 0.0, coeffs, 0.0).astype(BF)
        for j in range(PLANE):
            send_out[j, rows, :] = coeffs[:, j * TILE : (j + 1) * TILE]
            for part in range(2):
                to = pl.ds((1 + part) * LINE_USERS + s * USERS, USERS)
                send_out[j, to, :] = rounded[:, part * TILE : (part + 1) * TILE]


def owner_kernel(got_ref, out_ref, coeffs, rounded):
    for p in range(PLANE):
        users = slice(p * LINE_USERS, (p + 1) * LINE_USERS)
        coeffs[:, users] = got_ref[p, :LINE_USERS, :].astype(F32).T
        rounded[users, :TILE] = got_ref[p, LINE_USERS : 2 * LINE_USERS, :]
        rounded[users, TILE:] = got_ref[p, 2 * LINE_USERS : 3 * LINE_USERS, :]
    asked = jnp.concatenate(
        [got_ref[p, 3 * LINE_USERS :, :].astype(F32)[:1] for p in range(PLANE)], axis=1
    )
    for t in range(out_ref.shape[0] // TILE):
        picked = jnp.where(asked == float(t), coeffs[...], 0.0).astype(BF)
        out_ref[t * TILE : (t + 1) * TILE, :] = jnp.dot(
            picked, rounded[...], preferred_element_type=F32
        )


def call(kernel, outs, operands, spaces, out_spaces, scratch, prefetch=0):
    memory = {"v": pltpu.VMEM, "a": pl.ANY}
    return pl.pallas_call(
        kernel,
        out_shape=outs,
        grid_spec=pltpu.PrefetchScalarGridSpec(
            num_scalar_prefetch=prefetch,
            grid=(1,),
            in_specs=[spec(memory[m]) for m in spaces],
            out_specs=[spec(memory[m]) for m in out_spaces],
            scratch_shapes=scratch,
        ),
        compiler_params=pltpu.CompilerParams(vmem_limit_bytes=VMEM_LIMIT),
    )(*operands)


def spec(space):
    return pl.BlockSpec(memory_space=space)


def shards(item_factors, user_factors, strengths, requests, user_slots):
    z, x, y, c = (lax.axis_index(name) for name in EVERY)
    shape = jax.ShapeDtypeStruct
    pay = jnp.concatenate(
        [
            strengths,
            user_factors,
            jnp.pad(user_slots, ((0, 0), (0, TILE - SLOTS))).astype(BF),
            jnp.broadcast_to(requests, (USERS, TILE)).astype(BF),
        ],
        axis=1,
    )
    half_rows = item_factors.shape[0] // 2
    half = lax.dynamic_slice_in_dim(item_factors, c * half_rows, half_rows, 0)
    near = [half] + [lax.ppermute(half, EVERY, ring_pairs(d, 0)) for d in (1, -1, 2)]

    def grow(value, k):
        return jnp.concatenate([value, line_permute(value, lambda s: s ^ k)], axis=0)

    first_two = grow(pay[None], 1)
    held = grow(first_two, 2)
    got = line_permute(held, lambda s: s ^ 6)
    block = shape((BLOCK_ROWS, RANK), BF)
    square = shape((RANK, RANK), F32)
    near_a, near_b, gram = call(
        join_kernel, [block, block, square], [*near, first_two], "vvvva", "vvv", []
    )
    up_a = lax.ppermute(near_a, EVERY, ring_pairs(1, 1))
    down_b = lax.ppermute(near_b, EVERY, ring_pairs(-1, 1))
    up_b = lax.ppermute(near_b, EVERY, ring_pairs(1, 1))
    down_a = lax.ppermute(near_a, EVERY, ring_pairs(-1, 1))
    far_a = lax.ppermute(up_a, EVERY, ring_pairs(1, 1))
    far_b = lax.ppermute(down_b, EVERY, ring_pairs(-1, 1))
    [rest] = call(
        rest_kernel,
        [shape((6 * BLOCK_ROWS, RANK), BF)],
        [up_a, up_b, down_a, down_b, far_a, far_b, got],
        "a" * 7,
        "v",
        [pltpu.SemaphoreType.DMA((6,))],
    )
    [gram_a] = call(gram_kernel, [square], [gram, rest], "vv", "v", [])
    own = [near_a, near_b, rest]
    other = [swap_cores(v) for v in own]
    gram_b = swap_cores(gram_a)
    place = z[None].astype(jnp.int32)
    vectors = shape((LINE_USERS, RANK), F32)
    halves = shape((HALF, RANK), F32)
    weights, start, asked, asked_rows = call(
        weights_kernel,
        [
            shape((LINE_USERS, PLANE_ITEMS), BF),
            vectors,
            shape((NZ, TILE), F32),
            shape((PLANE, LINE_USERS), F32),
        ],
        [place, held, got],
        "vv",
        "vvvv",
        [pltpu.VMEM((LINE_USERS, TILE), F32)],
        prefetch=1,
    )
    asked = lax.dynamic_slice(asked, (0, z * PLANE), (NZ, PLANE))
    tile = jnp.maximum(asked.astype(jnp.int32), 0)
    part_of = tile // 4
    j = jnp.arange(PLANE, dtype=jnp.int32)[None, :]
    along_x = (j // NY - x) % NX
    along_y = (j % NY - y) % NY
    first = jnp.where(part_of == 0, along_y, along_x)
    second = jnp.where(part_of == 0, along_x, along_y)

    def slot(delta):
        return jnp.where(delta == 3, 1, jnp.where(delta == 0, 0, delta + 1))

    first, second = slot(first), slot(second)
    row = jnp.where(part_of == c, 0, 64) + second * 16 + first * 4 + tile % 4
    row = row.reshape(-1)
    part = pltpu.VMEM(vectors.shape, F32)
    keep, give, gram, table = call(
        first_kernel,
        [halves, halves, shape((RANK, RANK), F32), shape((16 * BLOCK_ROWS, RANK), BF)],
        [row, place, start, weights, gram_a, gram_b, *own, *other],
        "vvvv" + "a" * BLOCKS,
        "vvvv",
        [part, pltpu.SemaphoreType.DMA((BLOCKS,))],
        prefetch=2,
    )
    residual, keep, give = call(
        second_kernel,
        [vectors, halves, halves],
        [row, place, *line_sum(keep, give), start, gram, weights, table],
        "v" * 6,
        "vvv",
        [part],
        prefetch=2,
    )
    value, direction, norm, curve = call(
        third_kernel,
        [vectors, vectors, shape((LINE_USERS, TILE), F32), shape((8, LINE_USERS), F32)],
        [row, place, *line_sum(keep, give), start, residual, gram, weights, table],
        "v" * 7,
        "vvvv",
        [part, pltpu.VMEM((LINE_USERS, TILE), F32)],
        prefetch=2,
    )
    for k in (1, 2, 6):
        curve = curve + line_permute(curve, lambda s: s ^ k)
    solved, send = call(
        fourth_kernel,
        [shape((USERS, RANK), F32), shape((PLANE, SEND_ROWS, TILE), BF)],
        [row, place, curve, value, direction, norm, weights, asked_rows, table],
        "v" * 7,
        "vv",
        [part],
        prefetch=2,
    )
    got = lax.all_to_all(send, ("x", "y"), split_axis=0, concat_axis=0, tiled=True)
    [sums] = call(
        owner_kernel,
        [shape(item_factors.shape, F32)],
        [got],
        "v",
        "v",
        [
            pltpu.VMEM((TILE, PLANE * LINE_USERS), F32),
            pltpu.VMEM((PLANE * LINE_USERS, RANK), BF),
        ],
    )
    return solved, sums + swap_cores(sums)


def solution(mesh):
    cut = Mesh(mesh.devices.reshape(NZ, NX, NY, 2), EVERY)
    every, owner = P(EVERY, None), P(("z", "x", "y"), None)
    return jax.shard_map(
        shards,
        mesh=cut,
        in_specs=(owner, every, every, every, every),
        out_specs=(every, owner),
        check_vma=False,
    )
```
